32 devices in a mesh: lon: 4 (over y, x), lat: 8 (over z, core).
Axes of the slice: x: 2, y: 2, z: 4, core: 2. Of those that a mesh axis runs over, the one named last changes fastest.
Arguments:
- velocity: float32 [3, 64, 96, 384], P(None, 'lon', 'lat'), may hold values from -6 to 6
- pressure_in: float32 [64, 96, 384], P('lon', 'lat')
- viscosity: float32 [64, 96, 384], P('lon', 'lat'), as said below
- body_force: float32 [3, 64, 96, 384], P(None, 'lon', 'lat'), may hold values from -60 to 60
- colour_order: int32 [8], replicated, may hold values from 0 to 7, each once
Outputs:
- velocity_out: float32 [3, 64, 96, 384], P(None, 'lon', 'lat')
- pressure_out: float32 [64, 96, 384], P('lon', 'lat')
The draws below stay inside these ranges and needn't reach their ends.
Inputs may be any that keep to these rules, and one draw needn't show every extreme that they name: colour_order names each of the 8 colours once. viscosity lies between 1 and 1000000.
All inputs are finite; a program needn't handle non-finite values.
Results may differ from the reference program's by a relative error of at most 0.0003.
Values sent between devices are 32-bit elements; how exact they have to be, the bound alone decides.
No kernel may reach another device: no remote copies, remote signals or barrier semaphores. Data moves between devices by JAX's collectives and lax.ppermute only.
A program may use at most 320 MiB of HBM per device.

```python
import math
import jax
import jax.numpy as jnp
from jax import lax

SWEEPS = 2
COLOURS = 8
NX = 64
NY = 96
NZ = 384


def shared_viscosity(key):
    viscous_key = jax.random.fold_in(key, 11)
    exponent = jax.random.uniform(viscous_key, (NX, NY, NZ), jnp.float32, 0.0, math.log(1000000.0))
    return jnp.exp(exponent)


def shared_pressure(key):
    wave_key = jax.random.fold_in(key, 23)
    noise_key = jax.random.fold_in(key, 37)
    phases = jax.random.uniform(jax.random.fold_in(wave_key, 1), (3,), jnp.float32, 0.0, 2.0 * math.pi)
    factors = jax.random.uniform(jax.random.fold_in(wave_key, 2), (3,), jnp.float32, 0.5, 1.0)
    lon_pos = jnp.arange(NX).astype(jnp.float32)
    lat_pos = jnp.arange(NY).astype(jnp.float32)
    rad_pos = jnp.arange(NZ).astype(jnp.float32)
    lon_wave = factors[0] * 10.0 * NX / (2.0 * math.pi) * jnp.cos(2.0 * math.pi * lon_pos / NX + phases[0])
    lat_wave = factors[1] * 10.0 * NY / (2.0 * math.pi) * jnp.cos(math.pi * lat_pos / NY + phases[1])
    rad_wave = factors[2] * 10.0 * NZ / (2.0 * math.pi) * jnp.cos(math.pi * rad_pos / NZ + phases[2])
    smooth_part = lon_wave[:, None, None] + lat_wave[None, :, None] + rad_wave[None, None, :]
    noise = 3.0 * jax.random.normal(noise_key, (NX, NY, NZ), jnp.float32)
    return smooth_part + noise


def draw_viscosity(key, part):
    return shared_viscosity(key)


def draw_pressure_in(key, part):
    return shared_pressure(key) / shared_viscosity(key)


def block_scale(own_key, shape, cuts, least, top_value):
    level = 1.0
    for position, blocks in cuts:
        steps = jax.random.uniform(jax.random.fold_in(jax.random.fold_in(own_key, 6), position), (blocks,), jnp.float32, least / len(cuts), top_value / len(cuts))
        level = level * jnp.repeat(jnp.exp(steps), shape[position] // blocks).reshape((-1,) + (1,) * (len(shape) - 1 - position))
    return level


def normal_values(own_key, shape, scale, most, cuts=(), kind=jnp.bfloat16):
    array = jax.random.normal(own_key, shape, jnp.float32) * scale
    if len(cuts) > 0:
        array = block_scale(own_key, shape, cuts, -0.22, 0.18) * array
    return jnp.clip(array, min=-most, max=most).astype(kind)


def setup_inputs(seed: int = 0) -> dict:
    splits = jax.random.split(jax.random.key(seed), 6)
    velocity = normal_values(splits[0], (3, NX, NY, NZ), 1.0, 6.0, ((1, 4), (2, 8)), jnp.float32)
    pressure_in = draw_pressure_in(jax.random.fold_in(splits[5], 71), 0)
    viscosity = draw_viscosity(jax.random.fold_in(splits[5], 71), 0)
    body_force = normal_values(splits[3], (3, NX, NY, NZ), 10.0, 60.0, ((1, 4), (2, 8)), jnp.float32)
    colour_order = jax.random.permutation(splits[4], COLOURS).astype(jnp.int32)
    return dict(velocity=velocity, pressure_in=pressure_in, viscosity=viscosity, body_force=body_force, colour_order=colour_order)


damping = 0.6
coarse_gain = 0.25
unit_steps = ((1, 0, 0), (0, 1, 0), (0, 0, 1))


def stencil_offsets():
    result = []
    for step_x in (-1, 0, 1):
        for step_y in (-1, 0, 1):
            for step_z in (-1, 0, 1):
                reach = abs(step_x) + abs(step_y) + abs(step_z)
                if reach > 0:
                    result.append((step_x, step_y, step_z, 0.5 ** (reach - 1)))
    return result


def slide(values, offset, axis_no):
    if offset == 0:
        return values
    extent = values.shape[axis_no]
    padding = [(0, 0)] * values.ndim
    if offset > 0:
        padding[axis_no] = (0, offset)
        return lax.slice_in_dim(jnp.pad(values, padding), offset, offset + extent, axis=axis_no)
    padding[axis_no] = (-offset, 0)
    return lax.slice_in_dim(jnp.pad(values, padding), 0, extent, axis=axis_no)


def moved(values, step_x, step_y, step_z):
    base = values.ndim - 3
    result = values
    if step_x != 0:
        result = jnp.roll(result, -step_x, axis=base)
    result = slide(result, step_y, base + 1)
    return slide(result, step_z, base + 2)


def blend(own_value, next_value):
    return 2.0 * own_value * next_value / (own_value + next_value)


def viscous_diagonal(viscous):
    running = jnp.zeros_like(viscous)
    for step_x, step_y, step_z, weight in stencil_offsets():
        running = running + weight * blend(viscous, moved(viscous, step_x, step_y, step_z))
    return running


def residuals(fields, viscous, diagonal, body_force):
    velocity = fields[:3]
    pressure = fields[3]
    applied = diagonal * velocity
    for step_x, step_y, step_z, weight in stencil_offsets():
        coupling = weight * blend(viscous, moved(viscous, step_x, step_y, step_z))
        applied = applied - coupling * moved(velocity, step_x, step_y, step_z)
    gradient = jnp.stack([moved(pressure, -unit_step[0], -unit_step[1], -unit_step[2]) - pressure for unit_step in unit_steps])
    momentum = body_force - applied - gradient
    continuity = jnp.zeros_like(pressure)
    for axis_no, unit_step in enumerate(unit_steps):
        continuity = continuity - (moved(velocity[axis_no], unit_step[0], unit_step[1], unit_step[2]) - velocity[axis_no])
    return momentum, continuity


def colour_step(fields, viscous, diagonal, inverse, weight_sum, body_force, chosen):
    momentum, continuity = residuals(fields, viscous, diagonal, body_force)
    scaled = momentum * inverse
    mismatch = -continuity
    for axis_no, unit_step in enumerate(unit_steps):
        mismatch = mismatch + moved(scaled[axis_no], unit_step[0], unit_step[1], unit_step[2]) - scaled[axis_no]
    change = chosen * mismatch / weight_sum
    updates = []
    for axis_no, unit_step in enumerate(unit_steps):
        before = moved(chosen, -unit_step[0], -unit_step[1], -unit_step[2])
        earlier = moved(change, -unit_step[0], -unit_step[1], -unit_step[2])
        updates.append(inverse * ((chosen + before) * momentum[axis_no] + change - earlier))
    velocity = fields[:3] + damping * jnp.stack(updates)
    pressure = fields[3] + damping * change
    return jnp.concatenate([velocity, pressure[None]], axis=0)


def colour_codes(shape):
    lon_parity = jnp.arange(shape[0], dtype=jnp.int32) % 2
    lat_parity = jnp.arange(shape[1], dtype=jnp.int32) % 2
    rad_parity = jnp.arange(shape[2], dtype=jnp.int32) % 2
    return lon_parity[:, None, None] + 2 * lat_parity[None, :, None] + 4 * rad_parity[None, None, :]


def reference(velocity, pressure_in, viscosity, body_force, colour_order):
    diagonal = viscous_diagonal(viscosity)
    inverse = 1.0 / diagonal
    weight_sum = 3.0 * inverse
    for unit_step in unit_steps:
        weight_sum = weight_sum + moved(inverse, unit_step[0], unit_step[1], unit_step[2])
    parity_code = colour_codes(viscosity.shape)
    fields = jnp.concatenate([velocity, (pressure_in * viscosity)[None]], axis=0)

    def sweep(sweep_no, current):
        colour = colour_order[sweep_no % COLOURS]
        chosen = (parity_code == colour).astype(jnp.float32)
        return colour_step(current, viscosity, diagonal, inverse, weight_sum, body_force, chosen)

    fields = lax.fori_loop(0, SWEEPS * COLOURS, sweep, fields)
    momentum, continuity = residuals(fields, viscosity, diagonal, body_force)
    cycle_cells = NX // 8
    summed = momentum.reshape(3, cycle_cells, 8, NY // 4, 4, NZ // 4, 4).sum(axis=(2, 4, 6))
    viscous_sum = viscosity.reshape(cycle_cells, 8, NY // 4, 4, NZ // 4, 4).sum(axis=(1, 3, 5))
    coarse = summed / viscous_sum[None]
    decay_rate = 4.0 / cycle_cells
    screening = 2.0 * math.cosh(decay_rate) - 2.0
    angles = 2.0 * math.pi * jnp.arange(cycle_cells).astype(jnp.float32) / cycle_cells
    symbol = screening / (screening + 2.0 - 2.0 * jnp.cos(angles))
    spectrum = jnp.fft.fft(coarse, axis=1) * symbol[None, :, None, None]
    smooth = jnp.real(jnp.fft.ifft(spectrum, axis=1))
    spread = jnp.repeat(jnp.repeat(jnp.repeat(smooth, 8, axis=1), 4, axis=2), 4, axis=3)
    velocity_out = fields[:3] + coarse_gain * spread
    pressure_out = fields[3] / viscosity
    return velocity_out, pressure_out
```

```python
import functools
import math

import jax
import jax.numpy as jnp
from jax import lax
from jax.experimental import pallas as pl
from jax.experimental.pallas import tpu as pltpu
from jax.sharding import PartitionSpec as P

SWEEPS = 2
COLOURS = 8
damping = 0.6
coarse_gain = 0.25

HALF = 64
LANES = 128
SUBLANES = 16
Z_MARGIN = 16
Y_ROWS = 4
PARITIES = [(py, px, pz) for py in (0, 1) for px in (0, 1) for pz in (0, 1)]
OFFSETS = [
    (oy, ox, oz, 0.5 ** (abs(oy) + abs(ox) + abs(oz) - 1))
    for oy in (-1, 0, 1)
    for ox in (-1, 0, 1)
    for oz in (-1, 0, 1)
    if (oy, ox, oz) != (0, 0, 0)
]
STEPS = ((0, 1, 0), (1, 0, 0), (0, 0, 1))
VMEM = pl.BlockSpec(memory_space=pltpu.VMEM)
SMEM = pl.BlockSpec(memory_space=pltpu.SMEM)


def neighbour(parity, offset):
    py, px, pz = parity
    oy, ox, oz = offset[:3]
    shift = -1 if (py == 0 and oy == -1) else 1 if (py == 1 and oy == 1) else 0
    x_moved = (px == 0 and ox == -1) or (px == 1 and ox == 1)
    z_moved = (pz == 0 and oz == -1) or (pz == 1 and oz == 1)
    return shift, int(x_moved) + 2 * int(z_moved), (py ^ (oy & 1), px ^ (ox & 1), pz ^ (oz & 1))


def moved_x(value, px):
    rows = value.shape[0]
    number = lax.broadcasted_iota(jnp.int32, value.shape, 0)
    if px == 0:
        turned = pltpu.roll(value, rows - 1, 0)
        edge = number == rows - 1
    else:
        turned = pltpu.roll(value, 1, 0)
        edge = number == 0
    return jnp.where(edge, pltpu.roll(turned, HALF, 1), turned)


def moved_z(value, pz):
    return pltpu.roll(value, LANES - 1 if pz == 0 else 1, 1)


def at(j):
    return pl.ds(pl.multiple_of(j * SUBLANES, SUBLANES), SUBLANES)


def pitch(rows):
    return rows * SUBLANES + 8


def gathered(sums, parity):
    py, px, pz = parity
    along_x = sums[1] + moved_z(sums[3], 1 - pz)
    return sums[0] + moved_x(along_x, 1 - px) + moved_z(sums[2], 1 - pz)


def lower_lanes(shape):
    return lax.broadcasted_iota(jnp.int32, shape, len(shape) - 1) < HALF


def assemble_kernel(in_ref, state_ref, state_up_ref, state_down_ref, fixed_ref, fixed_up_ref, fixed_down_ref):
    rows = in_ref.shape[3]

    def one(j, carry):
        for f in range(8):
            own_ref = state_ref if f < 4 else fixed_ref
            for py in (0, 1):
                for px in (0, 1):
                    for t in (0, 1):
                        a = in_ref[t, f, py, j, px]
                        b = in_ref[t + 2, f, py, j, px]
                        low = lower_lanes(a.shape)
                        even = jnp.where(low, a, pltpu.roll(b, HALF, 1))
                        odd = jnp.where(low, pltpu.roll(a, HALF, 1), b)
                        own_ref[f % 4, py, j, px, 0, 8 * t : 8 * t + 8] = even
                        own_ref[f % 4, py, j, px, 1, 8 * t : 8 * t + 8] = odd
        return carry

    lax.fori_loop(0, rows, one, 0)
    for own_ref, up_ref, down_ref in (
        (state_ref, state_up_ref, state_down_ref), (fixed_ref, fixed_up_ref, fixed_down_ref)
    ):
        for f in range(4):
            for py in (0, 1):
                down_ref[f, py] = own_ref[f, py, 0:Y_ROWS]
                up_ref[f, py] = own_ref[f, py, rows - Y_ROWS : rows]


def place_rows(source, target_ref, fields, first, count):
    def one(j, carry):
        for py, px, pz in PARITIES:
            for f, g in fields:
                target_ref[g, py, px, pz, at(first + j)] = source[f, py, j, px, pz]
        return carry

    lax.fori_loop(0, count, one, 0)


def coupling_kernel(own_ref, below_ref, above_ref, *refs):
    c_refs = refs[:8]
    d_ref, f_ref, vs_ref, v_ref = refs[8:]
    rows = own_ref.shape[2]
    total = rows + 2 * Y_ROWS
    zero = jnp.zeros(own_ref.shape[-2:], jnp.float32)
    for py, px, pz in PARITIES:
        v_ref[0, py, px, pz, at(0)] = zero
        v_ref[0, py, px, pz, at(total + 1)] = zero
    for source, first, count in (
        (below_ref, 0, Y_ROWS), (own_ref, Y_ROWS, rows), (above_ref, Y_ROWS + rows, Y_ROWS)
    ):
        place_rows(source, f_ref, ((0, 0), (1, 1), (2, 2)), first, count)
        place_rows(source, v_ref, ((3, 0),), first + 1, count)

    def couple(j, carry):
        for parity in PARITIES:
            py, px, pz = parity
            mine = v_ref[0, py, px, pz, at(j + 1)]
            along_z = moved_z(mine, pz)
            seen = [mine, moved_x(mine, px), along_z, moved_x(along_z, px)]
            sums = [zero] * 4
            for n, offset in enumerate(OFFSETS):
                shift, variant, (ny, nx, nz) = neighbour(parity, offset)
                other = v_ref[0, ny, nx, nz, at(j + 1 + shift)]
                value = (2.0 * offset[3]) * seen[variant] * other / jnp.maximum(seen[variant] + other, 1.0)
                c_refs[4 * py + 2 * px + pz][n, at(j)] = value
                sums[variant] = sums[variant] + value
            running = gathered(sums, parity)
            d_ref[0, py, px, pz, at(j)] = running
            positive = (running > 0) & (mine > 0)
            d_ref[1, py, px, pz, at(j)] = jnp.where(positive, 1.0 / jnp.where(positive, running, 1.0), 0.0)
        return carry

    lax.fori_loop(0, total, couple, 0)

    def weigh(j, carry):
        for parity in PARITIES:
            py, px, pz = parity
            raw = 3.0 * d_ref[1, py, px, pz, at(j)]
            for step in STEPS:
                shift, variant, (ny, nx, nz) = neighbour(parity, step)
                other = d_ref[1, ny, nx, nz, at(j + shift)]
                if variant == 1:
                    other = moved_x(other, nx)
                elif variant == 2:
                    other = moved_z(other, nz)
                raw = raw + other
            inside = (v_ref[0, py, px, pz, at(j + 1)] > 0) & (raw > 0)
            d_ref[2, py, px, pz, at(j)] = jnp.where(inside, 1.0 / jnp.where(inside, raw, 1.0), 0.0)
        return carry

    lax.fori_loop(0, total - 1, weigh, 0)
    for py, px, pz in PARITIES:
        d_ref[2, py, px, pz, at(total - 1)] = zero
    for y in range(rows // 2):
        running = zero
        for j in (2 * y, 2 * y + 1):
            for py, px, pz in PARITIES:
                running = running + own_ref[3, py, j, px, pz]
        vs_ref[y] = running


def partial_momentum(u_ref, c_refs, d_ref, f_ref, parity, components, j):
    py, px, pz = parity
    sums = []
    p_here = u_ref[3, py, px, pz, at(j)]
    diagonal = d_ref[0, py, px, pz, at(j)]
    for d in components:
        first = f_ref[d, py, px, pz, at(j)] + p_here - diagonal * u_ref[d, py, px, pz, at(j)]
        sums.append([first, None, None, None])
    for n, offset in enumerate(OFFSETS):
        shift, variant, (ny, nx, nz) = neighbour(parity, offset)
        weight = c_refs[4 * py + 2 * px + pz][n, at(j)]
        for i, d in enumerate(components):
            value = weight * u_ref[d, ny, nx, nz, at(j + shift)]
            if offset[:3] == tuple(-s for s in STEPS[d]):
                value = value - u_ref[3, ny, nx, nz, at(j + shift)]
            sums[i][variant] = value if sums[i][variant] is None else sums[i][variant] + value
    return sums


def sweep_colour(colour, u_ref, c_refs, d_ref, f_ref, delta_ref, sums_ref, low, high):
    parity = (colour // 2 % 2, colour % 2, colour // 4)
    py, px, pz = parity
    faces = [neighbour(parity, step) for step in STEPS]

    def add_up(j):
        found = partial_momentum(u_ref, c_refs, d_ref, f_ref, parity, (0, 1, 2), j)
        for d, (shift, variant, face) in enumerate(faces):
            found += partial_momentum(u_ref, c_refs, d_ref, f_ref, face, (d,), j + shift)
        for i, sums in enumerate(found):
            for v in range(4):
                sums_ref[i, v] = sums[v]

    def change_row(j):
        here = [gathered([sums_ref[d, v] for v in range(4)], parity) for d in range(3)]
        there = [gathered([sums_ref[3 + d, v] for v in range(4)], faces[d][2]) for d in range(3)]
        inverse = d_ref[1, py, px, pz, at(j)]
        inverse_there = []
        total = None
        for d, (shift, variant, face) in enumerate(faces):
            inverse_there.append(d_ref[(1,) + face + (at(j + shift),)])
            term = there[d] * inverse_there[d] + u_ref[(d,) + face + (at(j + shift),)]
            if variant == 1:
                term = moved_x(term, face[1])
            elif variant == 2:
                term = moved_z(term, face[2])
            term = term - here[d] * inverse - u_ref[d, py, px, pz, at(j)]
            total = term if total is None else total + term
        weight = d_ref[2, py, px, pz, at(j)]
        change = total * weight
        for d, (shift, variant, face) in enumerate(faces):
            delta_ref[d, at(j)] = damping * inverse * (here[d] + change)
            back = change
            if variant == 1:
                back = moved_x(change, px)
            elif variant == 2:
                back = moved_z(change, pz)
            own = there[d]
            if d == 1 and py == 1:
                own = jnp.where(weight > 0, own, 0.0)
            if d == 2 and pz == 1:
                own = jnp.where(moved_z(weight, pz) > 0, own, 0.0)
            delta_ref[3 + d, at(j)] = damping * inverse_there[d] * (own - back)
        delta_ref[6, at(j)] = damping * change

    def work(j, carry):
        change_row(j - 1)
        add_up(j)
        return carry

    def apply(j, carry):
        for d, (shift, variant, face) in enumerate(faces):
            u_ref[d, py, px, pz, at(j)] += delta_ref[d, at(j)]
            u_ref[(d,) + face + (at(j + shift),)] += delta_ref[3 + d, at(j)]
        u_ref[3, py, px, pz, at(j)] += delta_ref[6, at(j)]
        return carry

    add_up(low)
    lax.fori_loop(low + 1, high, work, 0)
    change_row(high - 1)
    lax.fori_loop(low, high, apply, 0)


def group_bounds(order_ref, group):
    spoiled = 0
    for n in range(COLOURS // 2, COLOURS):
        spoiled = spoiled + order_ref[n] // 2 % 2
    cut = jnp.where(spoiled == 0, 13, 12)
    return ((0, 4), (4, 8), (8, cut), (cut, SWEEPS * COLOURS))[group]


def run_sweeps(group, order_ref, u_ref, c_refs, d_ref, f_ref, delta_ref, sums_ref, rows):
    first, end = group_bounds(order_ref, group)
    last = int(group == 3)

    def one(n, carry):
        colour = order_ref[n % COLOURS]
        later = end - 1 - n
        for k in range(COLOURS):
            ky = k // 2 % 2

            @pl.when(colour == k)
            def _(k=k, ky=ky):
                low = jnp.maximum(Y_ROWS - 1 - later + (1 - ky) * (1 - last), 1 - ky)
                high = jnp.minimum(Y_ROWS + rows + later + last, 2 * Y_ROWS + rows - 1)
                sweep_colour(k, u_ref, c_refs, d_ref, f_ref, delta_ref, sums_ref, low, high)

        return carry

    lax.fori_loop(first, end, one, 0)


def write_strips(u_ref, up_ref, down_ref, rows):
    def strip(j, carry):
        for py, px, pz in PARITIES:
            for f in range(4):
                down_ref[f, py, j, px, pz] = u_ref[f, py, px, pz, at(Y_ROWS + j)]
                up_ref[f, py, j, px, pz] = u_ref[f, py, px, pz, at(rows + j)]
        return carry

    lax.fori_loop(0, Y_ROWS, strip, 0)


def load_margins(below_ref, above_ref, u_ref, rows):
    fields = tuple((f, f) for f in range(4))
    place_rows(below_ref, u_ref, fields, 0, Y_ROWS)
    place_rows(above_ref, u_ref, fields, Y_ROWS + rows, Y_ROWS)


def first_kernel(order_ref, own_ref, below_ref, above_ref, *refs):
    c_refs = refs[:8]
    d_ref, f_ref, u_ref, up_ref, down_ref, delta_ref, sums_ref = refs[8:]
    rows = own_ref.shape[2]
    place_rows(own_ref, u_ref, tuple((f, f) for f in range(4)), Y_ROWS, rows)
    load_margins(below_ref, above_ref, u_ref, rows)
    run_sweeps(0, order_ref, u_ref, c_refs, d_ref, f_ref, delta_ref, sums_ref, rows)
    write_strips(u_ref, up_ref, down_ref, rows)


def sweep_kernel(group, order_ref, old_ref, below_ref, above_ref, *refs):
    c_refs = refs[:8]
    d_ref, f_ref, u_ref, up_ref, down_ref, delta_ref, sums_ref = refs[8:]
    rows = u_ref.shape[-2] // SUBLANES - 2 * Y_ROWS
    load_margins(below_ref, above_ref, u_ref, rows)
    run_sweeps(group, order_ref, u_ref, c_refs, d_ref, f_ref, delta_ref, sums_ref, rows)
    write_strips(u_ref, up_ref, down_ref, rows)


def pair_sum(value, axis, reach):
    size = value.shape[axis]
    number = lax.broadcasted_iota(jnp.int32, value.shape, axis)
    low = (number // reach) % 2 == 0
    partner = jnp.where(low, pltpu.roll(value, size - reach, axis), pltpu.roll(value, reach, axis))
    return value + partner


def coarse_sum(value):
    return pair_sum(pair_sum(pair_sum(value, 1, 1), 0, 1), 0, 2)


def cycle_weights(cells):
    rate = 4.0 / cells
    screening = 2.0 * math.cosh(rate) - 2.0
    factor = screening / (2.0 * math.sinh(rate) * math.sinh(rate * cells / 2.0))
    return [factor * math.cosh(rate * (cells / 2.0 - k)) for k in range(cells)]


def final_kernel(order_ref, old_ref, below_ref, above_ref, *refs):
    c_refs = refs[:8]
    d_ref, f_ref, vs_ref, u_ref, out_ref, delta_ref, sums_ref, sum_ref = refs[8:]
    rows = u_ref.shape[-2] // SUBLANES - 2 * Y_ROWS
    load_margins(below_ref, above_ref, u_ref, rows)
    run_sweeps(3, order_ref, u_ref, c_refs, d_ref, f_ref, delta_ref, sums_ref, rows)
    sum_ref[...] = jnp.zeros(sum_ref.shape, jnp.float32)

    def residual(j, carry):
        y = j // 2
        for parity in PARITIES:
            found = partial_momentum(u_ref, c_refs, d_ref, f_ref, parity, (0, 1, 2), Y_ROWS + j)
            for d in range(3):
                sum_ref[d, y] = sum_ref[d, y] + gathered(found[d], parity)
        return carry

    lax.fori_loop(0, rows, residual, 0)
    sublanes = SUBLANES
    cells = 2 * sublanes // 4
    weights = cycle_weights(cells)
    number = lax.broadcasted_iota(jnp.int32, (SUBLANES, LANES), 0)
    for y in range(rows // 2):
        viscous = coarse_sum(vs_ref[y])
        viscous = jnp.where(viscous > 0, viscous, 1.0)
        for d in range(3):
            coarse = coarse_sum(sum_ref[d, y]) / viscous
            smooth = weights[0] * coarse
            for k in range(1, cells):
                turned = pltpu.roll(coarse, sublanes - 4, 0)
                coarse = jnp.where(number >= sublanes - 4, pltpu.roll(turned, HALF, 1), turned)
                smooth = smooth + weights[k] * coarse
            sum_ref[d, y] = coarse_gain * smooth

    def pack(j, carry):
        for py in (0, 1):
            for px in (0, 1):
                for f in range(4):
                    even = u_ref[f, py, px, 0, at(Y_ROWS + j)]
                    odd = u_ref[f, py, px, 1, at(Y_ROWS + j)]
                    if f < 3:
                        added = sum_ref[f, j // 2]
                        even = even + added
                        odd = odd + added
                    low = lower_lanes(even.shape)
                    first = jnp.where(low, even, pltpu.roll(odd, HALF, 1))
                    second = jnp.where(low, pltpu.roll(even, HALF, 1), odd)
                    for t in (0, 1):
                        out_ref[t, f, py, j, px] = first[8 * t : 8 * t + 8]
                        out_ref[t + 2, f, py, j, px] = second[8 * t : 8 * t + 8]
        return carry

    lax.fori_loop(0, rows, pack, 0)


def refresh_pack_kernel(u_ref, left_ref, right_ref):
    rows = u_ref.shape[-2] // SUBLANES - 2 * Y_ROWS
    pairs = Z_MARGIN // 2
    lane = lax.broadcasted_iota(jnp.int32, (SUBLANES, LANES), 1) % HALF

    def one(j, carry):
        for py in (0, 1):
            for px in (0, 1):
                to_left = jnp.zeros((SUBLANES, LANES), jnp.float32)
                to_right = to_left
                for f in range(4):
                    for pz in (0, 1):
                        slot = 2 * f + pz
                        value = u_ref[f, py, px, pz, at(Y_ROWS + j)]
                        mine = (lane >= slot * pairs) & (lane < (slot + 1) * pairs)
                        to_left = jnp.where(mine, pltpu.roll(value, (slot * pairs - pairs) % LANES, 1), to_left)
                        to_right = jnp.where(
                            mine, pltpu.roll(value, (slot * pairs - (HALF - 2 * pairs)) % LANES, 1), to_right
                        )
                left_ref[py, j, px] = to_left
                right_ref[py, j, px] = to_right
        return carry

    lax.fori_loop(0, rows, one, 0)


def refresh_kernel(old_ref, from_left_ref, from_right_ref, u_ref, up_ref, down_ref):
    rows = u_ref.shape[-2] // SUBLANES - 2 * Y_ROWS
    pairs = Z_MARGIN // 2
    lane = lax.broadcasted_iota(jnp.int32, (SUBLANES, LANES), 1) % HALF

    def one(j, carry):
        for py in (0, 1):
            for px in (0, 1):
                low = from_left_ref[py, j, px]
                high = from_right_ref[py, j, px]
                for f in range(4):
                    for pz in (0, 1):
                        slot = 2 * f + pz
                        value = u_ref[f, py, px, pz, at(Y_ROWS + j)]
                        value = jnp.where(lane < pairs, pltpu.roll(low, (-slot * pairs) % LANES, 1), value)
                        value = jnp.where(
                            lane >= HALF - pairs,
                            pltpu.roll(high, (HALF - pairs - slot * pairs) % LANES, 1),
                            value,
                        )
                        u_ref[f, py, px, pz, at(Y_ROWS + j)] = value
        return carry

    lax.fori_loop(0, rows, one, 0)
    write_strips(u_ref, up_ref, down_ref, rows)


def cut_windows(pieces, out_ref, place, parts):
    shape = pieces[0].shape
    tiles = len(pieces)
    width = tiles * LANES // parts
    lane = lax.broadcasted_iota(jnp.int32, shape, 1)
    order = 2 * (lane % HALF) + lane // HALF
    pieces = [jnp.take_along_axis(piece, order, axis=1) for piece in pieces]
    pair = lane % HALF
    for s in range(parts):
        start = (width * s - Z_MARGIN) // 2
        first, offset = start // HALF, start % HALF
        found = jnp.zeros(shape, jnp.float32)
        if 0 <= first < tiles:
            found = jnp.where(pair < HALF - offset, pltpu.roll(pieces[first], (-offset) % LANES, 1), found)
        if 0 <= first + 1 < tiles:
            found = jnp.where(pair >= HALF - offset, pltpu.roll(pieces[first + 1], (HALF - offset) % LANES, 1), found)
        if width + 2 * Z_MARGIN < LANES:
            found = jnp.where(pair < width // 2 + Z_MARGIN, found, 0.0)
        out_ref[(s,) + place] = found


def pack_kernel(velocity_ref, pressure_ref, viscosity_ref, force_ref, out_ref, row_ref):
    parts, _, _, rows = out_ref.shape[:4]
    half = out_ref.shape[5]
    tiles = row_ref.shape[2]

    def one(j, carry):
        for py in (0, 1):
            y = 2 * j + py
            for t in range(tiles):
                columns = slice(LANES * t, LANES * (t + 1))
                viscous = viscosity_ref[y, :, columns]
                row_ref[py, 7, t] = viscous
                row_ref[py, 3, t] = viscous * pressure_ref[y, :, columns]
                for d in range(3):
                    row_ref[py, d, t] = velocity_ref[d, y, :, columns]
                    row_ref[py, 4 + d, t] = force_ref[d, y, :, columns]
        for py in (0, 1):
            for px in (0, 1):
                for f in range(8):
                    pieces = [row_ref[py, f, t, pl.ds(px, half, stride=2), :] for t in range(tiles)]
                    cut_windows(pieces, out_ref, (f, py, j, px), parts)
        return carry

    lax.fori_loop(0, rows, one, 0)


def unpack_kernel(back_ref, viscosity_ref, velocity_ref, pressure_ref, row_ref):
    parts, fields, _, rows = back_ref.shape[:4]
    tiles = row_ref.shape[2]
    width = tiles * LANES // parts
    shape = back_ref.shape[-2:]
    lane = lax.broadcasted_iota(jnp.int32, shape, 1)
    order = HALF * (lane % 2) + lane // 2

    def one(j, carry):
        for py in (0, 1):
            for px in (0, 1):
                for f in range(fields):
                    pieces = [jnp.zeros(shape, jnp.float32)] * tiles
                    for s in range(parts):
                        start = width * s - Z_MARGIN
                        found = jnp.take_along_axis(back_ref[s, f, py, j, px], order, axis=1)
                        found = pltpu.roll(found, start % LANES, 1)
                        for t in range(tiles):
                            low = max(width * s - LANES * t, 0)
                            high = min(width * (s + 1) - LANES * t, LANES)
                            if low < high:
                                pieces[t] = jnp.where((lane >= low) & (lane < high), found, pieces[t])
                    for t, piece in enumerate(pieces):
                        row_ref[py, f, t, pl.ds(px, shape[0], stride=2), :] = piece
        for py in (0, 1):
            y = 2 * j + py
            for t in range(tiles):
                columns = slice(LANES * t, LANES * (t + 1))
                for d in range(3):
                    velocity_ref[d, y, :, columns] = row_ref[py, d, t]
                pressure_ref[y, :, columns] = row_ref[py, 3, t] / viscosity_ref[y, :, columns]
        return carry

    lax.fori_loop(0, rows, one, 0)


def shaped(*shape):
    return jax.ShapeDtypeStruct(shape, jnp.float32)


def kept(*shape):
    return pltpu.VMEM(shape, jnp.float32)


def hold(value):
    return pltpu.with_memory_space_constraint(value, pltpu.VMEM)


def params(mib):
    return pltpu.CompilerParams(vmem_limit_bytes=mib * 2**20)


def exchange(value_up, value_down, axis, count):
    below = lax.ppermute(value_up, axis, [(i, i + 1) for i in range(count - 1)])
    above = lax.ppermute(value_down, axis, [(i + 1, i) for i in range(count - 1)])
    return below, above


def body_windows(velocity, pressure_in, viscosity, body_force, colour_order):
    lon_cells, lat_cells, rad_cells = viscosity.shape
    parts = lax.axis_size("lon")
    lats = lax.axis_size("lat")
    rows = lat_cells // 2
    total = rows + 2 * Y_ROWS
    tile = (SUBLANES, LANES)
    own = shaped(4, 2, rows, 2, 2, *tile)
    strip = shaped(4, 2, Y_ROWS, 2, 2, *tile)
    sent = pl.pallas_call(
        pack_kernel,
        out_shape=shaped(parts, 8, 2, rows, 2, lon_cells // 2, LANES),
        in_specs=[VMEM] * 4,
        out_specs=VMEM,
        scratch_shapes=[pltpu.VMEM((2, 8, rad_cells // LANES, lon_cells, LANES), jnp.float32)],
        compiler_params=params(16),
    )(
        velocity.transpose(0, 2, 1, 3), pressure_in.transpose(1, 0, 2),
        viscosity.transpose(1, 0, 2), body_force.transpose(0, 2, 1, 3),
    )
    got = lax.all_to_all(sent, "lon", 0, 0, tiled=True)
    own_state, state_up, state_down, own_fixed, fixed_up, fixed_down = pl.pallas_call(
        assemble_kernel,
        out_shape=(own, strip, strip) * 2,
        in_specs=[VMEM],
        out_specs=(VMEM,) * 6,
        compiler_params=params(16),
    )(got)
    fixed_below, fixed_above = exchange(fixed_up, fixed_down, "lat", lats)
    below, above = exchange(state_up, state_down, "lat", lats)
    stacked = (2, 2, 2)
    *couplings, diagonals, force, viscous_sum = pl.pallas_call(
        coupling_kernel,
        out_shape=(
            *[kept(len(OFFSETS), pitch(total), LANES)] * 8,
            kept(3, *stacked, pitch(total), LANES),
            kept(3, *stacked, pitch(total), LANES),
            shaped(rows // 2, *tile),
        ),
        in_specs=[VMEM, VMEM, VMEM],
        out_specs=(VMEM,) * 11,
        scratch_shapes=[pltpu.VMEM((1,) + stacked + (pitch(total + 2), LANES), jnp.float32)],
        compiler_params=params(10),
    )(own_fixed, fixed_below, fixed_above)
    constants = [hold(array) for array in (*couplings, diagonals, force)]
    state_type = kept(4, *stacked, pitch(total), LANES)
    scratch = [
        pltpu.VMEM((7, pitch(total), LANES), jnp.float32),
        pltpu.VMEM((6, 4) + tile, jnp.float32),
    ]
    state, up, down = pl.pallas_call(
        first_kernel,
        out_shape=(state_type, strip, strip),
        in_specs=[SMEM] + [VMEM] * 13,
        out_specs=(VMEM, VMEM, VMEM),
        scratch_shapes=scratch,
        compiler_params=params(8),
    )(colour_order, own_state, below, above, *constants)
    for g in (1, 2):
        below, above = exchange(up, down, "lat", lats)
        state, up, down = pl.pallas_call(
            functools.partial(sweep_kernel, g),
            out_shape=(state_type, strip, strip),
            in_specs=[SMEM] + [VMEM] * 13,
            out_specs=(VMEM, VMEM, VMEM),
            scratch_shapes=scratch,
            input_output_aliases={1: 0},
            compiler_params=params(8),
        )(colour_order, hold(state), below, above, *constants)
        if g == 1:
            packed = shaped(2, rows, 2, *tile)
            to_left, to_right = pl.pallas_call(
                refresh_pack_kernel,
                out_shape=(packed, packed),
                in_specs=[VMEM],
                out_specs=(VMEM, VMEM),
                compiler_params=params(6),
            )(hold(state))
            from_left, from_right = exchange(to_right, to_left, "lon", parts)
            state, up, down = pl.pallas_call(
                refresh_kernel,
                out_shape=(state_type, strip, strip),
                in_specs=[VMEM] * 3,
                out_specs=(VMEM, VMEM, VMEM),
                input_output_aliases={0: 0},
                compiler_params=params(6),
            )(hold(state), from_left, from_right)
    below, above = exchange(up, down, "lat", lats)
    state, packed = pl.pallas_call(
        final_kernel,
        out_shape=(state_type, shaped(parts, 4, 2, rows, 2, lon_cells // 2, LANES)),
        in_specs=[SMEM] + [VMEM] * 14,
        out_specs=(VMEM, VMEM),
        scratch_shapes=scratch + [pltpu.VMEM((3, rows // 2) + tile, jnp.float32)],
        input_output_aliases={1: 0},
        compiler_params=params(8),
    )(colour_order, hold(state), below, above, *constants, viscous_sum)
    back = lax.all_to_all(packed, "lon", 0, 0, tiled=True)
    velocity_out, pressure_out = pl.pallas_call(
        unpack_kernel,
        out_shape=(shaped(3, lat_cells, lon_cells, rad_cells), shaped(lat_cells, lon_cells, rad_cells)),
        in_specs=[VMEM, VMEM],
        out_specs=(VMEM, VMEM),
        scratch_shapes=[pltpu.VMEM((2, 4, rad_cells // LANES, lon_cells, LANES), jnp.float32)],
        compiler_params=params(16),
    )(back, viscosity.transpose(1, 0, 2))
    return velocity_out.transpose(0, 2, 1, 3), pressure_out.transpose(1, 0, 2)


unit_steps = ((1, 0, 0), (0, 1, 0), (0, 0, 1))


def extended_2(block, sides, width, periodic):
    for axis, dim in sides:
        count = lax.axis_size(axis)
        forward = [(i, i + 1) for i in range(count - 1)]
        if periodic:
            forward.append((count - 1, 0))
        backward = [(target, source) for source, target in forward]
        low = lax.ppermute(
            lax.slice_in_dim(block, block.shape[dim] - width, None, axis=dim), axis, forward
        )
        high = lax.ppermute(lax.slice_in_dim(block, 0, width, axis=dim), axis, backward)
        block = jnp.concatenate([low, block, high], axis=dim)
    return block


def stencil_offsets():
    result = []
    for step_x in (-1, 0, 1):
        for step_y in (-1, 0, 1):
            for step_z in (-1, 0, 1):
                reach = abs(step_x) + abs(step_y) + abs(step_z)
                if reach > 0:
                    result.append((step_x, step_y, step_z, 0.5 ** (reach - 1)))
    return result


def slide(values, offset, axis_no):
    if offset == 0:
        return values
    extent = values.shape[axis_no]
    padding = [(0, 0)] * values.ndim
    if offset > 0:
        padding[axis_no] = (0, offset)
        return lax.slice_in_dim(jnp.pad(values, padding), offset, offset + extent, axis=axis_no)
    padding[axis_no] = (-offset, 0)
    return lax.slice_in_dim(jnp.pad(values, padding), 0, extent, axis=axis_no)


def moved(values, step_x, step_y, step_z):
    base = values.ndim - 3
    result = slide(values, step_x, base)
    result = slide(result, step_y, base + 1)
    return slide(result, step_z, base + 2)


def blend(own_value, next_value):
    return 2.0 * own_value * next_value / jnp.maximum(own_value + next_value, 1.0)


def viscous_diagonal(viscous):
    running = jnp.zeros_like(viscous)
    for step_x, step_y, step_z, weight in stencil_offsets():
        running = running + weight * blend(viscous, moved(viscous, step_x, step_y, step_z))
    return running


def residuals(fields, viscous, diagonal, body_force):
    velocity = fields[:3]
    pressure = fields[3]
    applied = diagonal * velocity
    for step_x, step_y, step_z, weight in stencil_offsets():
        coupling = weight * blend(viscous, moved(viscous, step_x, step_y, step_z))
        applied = applied - coupling * moved(velocity, step_x, step_y, step_z)
    gradient = jnp.stack(
        [
            moved(pressure, -unit_step[0], -unit_step[1], -unit_step[2]) - pressure
            for unit_step in unit_steps
        ]
    )
    momentum = body_force - applied - gradient
    continuity = jnp.zeros_like(pressure)
    for axis_no, unit_step in enumerate(unit_steps):
        continuity = continuity - (
            moved(velocity[axis_no], unit_step[0], unit_step[1], unit_step[2]) - velocity[axis_no]
        )
    return (momentum, continuity)


def colour_step(fields, viscous, diagonal, inverse, weight_sum, body_force, chosen):
    momentum, continuity = residuals(fields, viscous, diagonal, body_force)
    scaled = momentum * inverse
    mismatch = -continuity
    for axis_no, unit_step in enumerate(unit_steps):
        mismatch = (
            mismatch
            + moved(scaled[axis_no], unit_step[0], unit_step[1], unit_step[2])
            - scaled[axis_no]
        )
    change = chosen * mismatch / weight_sum
    updates = []
    for axis_no, unit_step in enumerate(unit_steps):
        before = moved(chosen, -unit_step[0], -unit_step[1], -unit_step[2])
        earlier = moved(change, -unit_step[0], -unit_step[1], -unit_step[2])
        updates.append(inverse * ((chosen + before) * momentum[axis_no] + change - earlier))
    velocity = fields[:3] + damping * jnp.stack(updates)
    pressure = fields[3] + damping * change
    return jnp.concatenate([velocity, pressure[None]], axis=0)


def colour_codes(shape):
    lon_parity = jnp.arange(shape[0], dtype=jnp.int32) % 2
    lat_parity = jnp.arange(shape[1], dtype=jnp.int32) % 2
    rad_parity = jnp.arange(shape[2], dtype=jnp.int32) % 2
    return lon_parity[:, None, None] + 2 * lat_parity[None, :, None] + 4 * rad_parity[None, None, :]


def extend(fields, margin):
    beside_all = extended_2(fields, (("lon", 1),), margin, True)
    return extended_2(beside_all, (("lat", 2),), margin, False)


def cycle_kernel(distance, cycle_cells):
    decay_rate = 4.0 / cycle_cells
    screening = 2.0 * math.cosh(decay_rate) - 2.0
    factor = screening / (2.0 * math.sinh(decay_rate) * math.sinh(decay_rate * cycle_cells / 2.0))
    wrapped = jnp.mod(distance, cycle_cells).astype(jnp.float32)
    return factor * jnp.cosh(decay_rate * (cycle_cells / 2.0 - wrapped))


def body_general(velocity, pressure_in, viscosity, body_force, colour_order):
    groups = 1
    margin = 2 * groups
    lon_cells, lat_cells, rad_cells = viscosity.shape
    lat_total = lax.axis_size("lat") * lat_cells
    lat_global = (
        lax.axis_index("lat") * lat_cells
        - margin
        + jnp.arange(lat_cells + 2 * margin, dtype=jnp.int32)
    )
    inside_lat = ((lat_global >= 0) & (lat_global < lat_total)).astype(jnp.float32)
    inside = jnp.broadcast_to(
        inside_lat[None, :, None], (lon_cells + 2 * margin, lat_cells + 2 * margin, rad_cells)
    )
    constant_fields = jnp.concatenate([body_force, viscosity[None]], axis=0)
    constant_wide = extended_2(constant_fields, (("lon", 1), ("lat", 2)), margin, True) * inside
    force_wide = constant_wide[:3]
    viscous_wide = constant_wide[3]
    diagonal = viscous_diagonal(viscous_wide)
    inverse = jnp.where(inside > 0, 1.0 / jnp.where(diagonal > 0, diagonal, 1.0), 0.0)
    weight_raw = 3.0 * inverse
    for unit_step in unit_steps:
        weight_raw = weight_raw + moved(inverse, unit_step[0], unit_step[1], unit_step[2])
    weight_sum = jnp.where(weight_raw > 0, weight_raw, 1.0)
    parity_code = colour_codes(inside.shape)
    fields = jnp.concatenate([velocity, (pressure_in * viscosity)[None]], axis=0)

    def sweep_block(block_no, current):
        extended = extend(current, margin)
        colour = colour_order[(block_no * groups + 0) % COLOURS]
        chosen = (parity_code == colour).astype(jnp.float32) * inside
        extended = colour_step(
            extended, viscous_wide, diagonal, inverse, weight_sum, force_wide, chosen
        )
        return extended[:, margin : margin + lon_cells, margin : margin + lat_cells, :]

    fields = lax.fori_loop(0, SWEEPS * COLOURS // groups, sweep_block, fields)
    extended = extend(fields, margin)
    momentum, continuity = residuals(extended, viscous_wide, diagonal, force_wide)
    momentum = momentum[:, margin : margin + lon_cells, margin : margin + lat_cells, :]
    lon_coarse = lon_cells // 8
    lat_coarse = lat_cells // 4
    rad_coarse = rad_cells // 4
    cycle_cells = lax.axis_size("lon") * lon_coarse
    own_first = lax.axis_index("lon") * lon_coarse
    summed = momentum.reshape(3, lon_coarse, 8, lat_coarse, 4, rad_coarse, 4).sum(axis=(2, 4, 6))
    viscous_sum = viscosity.reshape(lon_coarse, 8, lat_coarse, 4, rad_coarse, 4).sum(axis=(1, 3, 5))
    coarse = jnp.transpose(summed / viscous_sum[None], (1, 0, 2, 3))
    shard_piece = lax.all_gather(coarse, "lon", axis=0, tiled=True)
    sources = jnp.arange(shard_piece.shape[0], dtype=jnp.int32)
    targets = own_first + jnp.arange(lon_coarse, dtype=jnp.int32)
    kernel_table = cycle_kernel(targets[None, :] - sources[:, None], cycle_cells)
    smooth = jnp.einsum("jcyz,ji->icyz", shard_piece, kernel_table, precision=lax.Precision.HIGHEST)
    smooth = jnp.transpose(smooth, (1, 0, 2, 3))
    spread = jnp.repeat(jnp.repeat(jnp.repeat(smooth, 8, axis=1), 4, axis=2), 4, axis=3)
    velocity_out = fields[:3] + coarse_gain * spread
    pressure_out = fields[3] / viscosity
    return (velocity_out, pressure_out)


def body(velocity, pressure_in, viscosity, body_force, colour_order):
    lon_cells, lat_cells, rad_cells = viscosity.shape
    parts = lax.axis_size("lon")
    fits = (
        parts == 4
        and parts * lon_cells == 4 * SUBLANES
        and lat_cells % 4 == 0
        and lat_cells >= 2 * Y_ROWS
        and rad_cells % LANES == 0
        and rad_cells % (4 * parts) == 0
        and rad_cells // parts + 2 * Z_MARGIN <= LANES
        and Z_MARGIN <= rad_cells // parts
    )
    chosen = body_windows if fits else body_general
    return chosen(velocity, pressure_in, viscosity, body_force, colour_order)


def solution(mesh):
    placed = (
        P(None, "lon", "lat", None),
        P("lon", "lat", None),
        P("lon", "lat", None),
        P(None, "lon", "lat", None),
        P(),
    )
    return jax.shard_map(
        body,
        mesh=mesh,
        in_specs=placed,
        out_specs=(P(None, "lon", "lat", None), P("lon", "lat", None)),
        check_vma=False,
    )
```

```python
import functools
import math

import jax
import jax.numpy as jnp
from jax import lax
from jax.experimental import pallas as pl
from jax.experimental.pallas import tpu as pltpu
from jax.sharding import PartitionSpec as P

SWEEPS = 2
COLOURS = 8
damping = 0.6
coarse_gain = 0.25

LANES = 128
SUBLANES = 16
Z_MARGIN = 16
Y_ROWS = 4
PARITIES = [(py, px, pz) for py in (0, 1) for px in (0, 1) for pz in (0, 1)]
OFFSETS = [
    (oy, ox, oz, 0.5 ** (abs(oy) + abs(ox) + abs(oz) - 1))
    for oy in (-1, 0, 1)
    for ox in (-1, 0, 1)
    for oz in (-1, 0, 1)
    if (oy, ox, oz) != (0, 0, 0)
]
STEPS = ((0, 1, 0), (1, 0, 0), (0, 0, 1))
VMEM = pl.BlockSpec(memory_space=pltpu.VMEM)
SMEM = pl.BlockSpec(memory_space=pltpu.SMEM)


def neighbour(parity, offset):
    py, px, pz = parity
    oy, ox, oz = offset[:3]
    shift = -1 if (py == 0 and oy == -1) else 1 if (py == 1 and oy == 1) else 0
    x_moved = (px == 0 and ox == -1) or (px == 1 and ox == 1)
    z_moved = (pz == 0 and oz == -1) or (pz == 1 and oz == 1)
    return shift, int(x_moved) + 2 * int(z_moved), (py ^ (oy & 1), px ^ (ox & 1), pz ^ (oz & 1))


def even_lanes(shape):
    return lax.broadcasted_iota(jnp.int32, shape, len(shape) - 1) % 2 == 0


def swapped(value):
    return jnp.where(even_lanes(value.shape), pltpu.roll(value, LANES - 1, 1), pltpu.roll(value, 1, 1))


def moved_x(value, px):
    rows = value.shape[0]
    number = lax.broadcasted_iota(jnp.int32, value.shape, 0)
    if px == 0:
        turned = pltpu.roll(value, rows - 1, 0)
        edge = number == rows - 1
    else:
        turned = pltpu.roll(value, 1, 0)
        edge = number == 0
    return jnp.where(edge, swapped(turned), turned)


def moved_z(value, pz):
    return pltpu.roll(value, LANES - 2 if pz == 0 else 2, 1)


def at(j):
    return pl.ds(pl.multiple_of(j * SUBLANES, SUBLANES), SUBLANES)


def pitch(rows):
    return rows * SUBLANES + 8


def gathered(sums, parity):
    py, px, pz = parity
    along_x = sums[1] + moved_z(sums[3], 1 - pz)
    return sums[0] + moved_x(along_x, 1 - px) + moved_z(sums[2], 1 - pz)


def assemble_kernel(in_ref, own_ref, up_ref, down_ref):
    fields, rows = own_ref.shape[0], own_ref.shape[2]

    def one(j, carry):
        for f in range(fields):
            for py in (0, 1):
                for px in (0, 1):
                    for t in (0, 1):
                        a = in_ref[t, f, py, j, px]
                        b = in_ref[t + 2, f, py, j, px]
                        low = even_lanes(a.shape)
                        even = jnp.where(low, a, pltpu.roll(b, 1, 1))
                        odd = jnp.where(low, pltpu.roll(a, LANES - 1, 1), b)
                        own_ref[f, py, j, px, 0, 8 * t : 8 * t + 8] = even
                        own_ref[f, py, j, px, 1, 8 * t : 8 * t + 8] = odd
        return carry

    lax.fori_loop(0, rows, one, 0)
    for f in range(fields):
        for py in (0, 1):
            down_ref[f, py] = own_ref[f, py, 0:Y_ROWS]
            up_ref[f, py] = own_ref[f, py, rows - Y_ROWS : rows]


def place_rows(source, target_ref, fields, first, count):
    def one(j, carry):
        for py, px, pz in PARITIES:
            for f, g in fields:
                target_ref[g, py, px, pz, at(first + j)] = source[f, py, j, px, pz]
        return carry

    lax.fori_loop(0, count, one, 0)


def coupling_kernel(own_ref, below_ref, above_ref, *refs):
    c_refs = refs[:8]
    d_ref, f_ref, vs_ref, v_ref = refs[8:]
    rows = own_ref.shape[2]
    total = rows + 2 * Y_ROWS
    zero = jnp.zeros(own_ref.shape[-2:], jnp.float32)
    for py, px, pz in PARITIES:
        v_ref[0, py, px, pz, at(0)] = zero
        v_ref[0, py, px, pz, at(total + 1)] = zero
    for source, first, count in (
        (below_ref, 0, Y_ROWS), (own_ref, Y_ROWS, rows), (above_ref, Y_ROWS + rows, Y_ROWS)
    ):
        place_rows(source, f_ref, ((0, 0), (1, 1), (2, 2)), first, count)
        place_rows(source, v_ref, ((3, 0),), first + 1, count)

    def couple(j, carry):
        for parity in PARITIES:
            py, px, pz = parity
            mine = v_ref[0, py, px, pz, at(j + 1)]
            along_z = moved_z(mine, pz)
            seen = [mine, moved_x(mine, px), along_z, moved_x(along_z, px)]
            sums = [zero] * 4
            for n, offset in enumerate(OFFSETS):
                shift, variant, (ny, nx, nz) = neighbour(parity, offset)
                other = v_ref[0, ny, nx, nz, at(j + 1 + shift)]
                value = (2.0 * offset[3]) * seen[variant] * other / jnp.maximum(seen[variant] + other, 1.0)
                c_refs[4 * py + 2 * px + pz][n, at(j)] = value
                sums[variant] = sums[variant] + value
            running = gathered(sums, parity)
            d_ref[0, py, px, pz, at(j)] = running
            positive = (running > 0) & (mine > 0)
            d_ref[1, py, px, pz, at(j)] = jnp.where(positive, 1.0 / jnp.where(positive, running, 1.0), 0.0)
        return carry

    lax.fori_loop(0, total, couple, 0)

    def weigh(j, carry):
        for parity in PARITIES:
            py, px, pz = parity
            raw = 3.0 * d_ref[1, py, px, pz, at(j)]
            for step in STEPS:
                shift, variant, (ny, nx, nz) = neighbour(parity, step)
                other = d_ref[1, ny, nx, nz, at(j + shift)]
                if variant == 1:
                    other = moved_x(other, nx)
                elif variant == 2:
                    other = moved_z(other, nz)
                raw = raw + other
            inside = (v_ref[0, py, px, pz, at(j + 1)] > 0) & (raw > 0)
            d_ref[2, py, px, pz, at(j)] = jnp.where(inside, 1.0 / jnp.where(inside, raw, 1.0), 0.0)
        return carry

    lax.fori_loop(0, total - 1, weigh, 0)
    for py, px, pz in PARITIES:
        d_ref[2, py, px, pz, at(total - 1)] = zero
    for y in range(rows // 2):
        running = zero
        for j in (2 * y, 2 * y + 1):
            for py, px, pz in PARITIES:
                running = running + own_ref[3, py, j, px, pz]
        vs_ref[y] = running


def partial_momentum(u_ref, c_refs, d_ref, f_ref, parity, components, j):
    py, px, pz = parity
    sums = []
    p_here = u_ref[3, py, px, pz, at(j)]
    diagonal = d_ref[0, py, px, pz, at(j)]
    for d in components:
        first = f_ref[d, py, px, pz, at(j)] + p_here - diagonal * u_ref[d, py, px, pz, at(j)]
        sums.append([first, None, None, None])
    for n, offset in enumerate(OFFSETS):
        shift, variant, (ny, nx, nz) = neighbour(parity, offset)
        weight = c_refs[4 * py + 2 * px + pz][n, at(j)]
        for i, d in enumerate(components):
            value = weight * u_ref[d, ny, nx, nz, at(j + shift)]
            if offset[:3] == tuple(-s for s in STEPS[d]):
                value = value - u_ref[3, ny, nx, nz, at(j + shift)]
            sums[i][variant] = value if sums[i][variant] is None else sums[i][variant] + value
    return sums


def sweep_colour(colour, u_ref, c_refs, d_ref, f_ref, delta_ref, sums_ref, low, high):
    parity = (colour // 2 % 2, colour % 2, colour // 4)
    py, px, pz = parity
    faces = [neighbour(parity, step) for step in STEPS]

    def add_up(j, slot):
        found = partial_momentum(u_ref, c_refs, d_ref, f_ref, parity, (0, 1, 2), j)
        for d, (shift, variant, face) in enumerate(faces):
            found += partial_momentum(u_ref, c_refs, d_ref, f_ref, face, (d,), j + shift)
        for i, sums in enumerate(found):
            for v in range(4):
                sums_ref[slot, i, v] = sums[v]

    def change_row(j, slot):
        here = [gathered([sums_ref[slot, d, v] for v in range(4)], parity) for d in range(3)]
        there = [gathered([sums_ref[slot, 3 + d, v] for v in range(4)], faces[d][2]) for d in range(3)]
        inverse = d_ref[1, py, px, pz, at(j)]
        inverse_there = []
        total = None
        for d, (shift, variant, face) in enumerate(faces):
            inverse_there.append(d_ref[(1,) + face + (at(j + shift),)])
            term = there[d] * inverse_there[d] + u_ref[(d,) + face + (at(j + shift),)]
            if variant == 1:
                term = moved_x(term, face[1])
            elif variant == 2:
                term = moved_z(term, face[2])
            term = term - here[d] * inverse - u_ref[d, py, px, pz, at(j)]
            total = term if total is None else total + term
        weight = d_ref[2, py, px, pz, at(j)]
        change = total * weight
        for d, (shift, variant, face) in enumerate(faces):
            delta_ref[d, at(j)] = damping * inverse * (here[d] + change)
            back = change
            if variant == 1:
                back = moved_x(change, px)
            elif variant == 2:
                back = moved_z(change, pz)
            own = there[d]
            if d == 1 and py == 1:
                own = jnp.where(weight > 0, own, 0.0)
            if d == 2 and pz == 1:
                own = jnp.where(moved_z(weight, pz) > 0, own, 0.0)
            delta_ref[3 + d, at(j)] = damping * inverse_there[d] * (own - back)
        delta_ref[6, at(j)] = damping * change

    def work(i, carry):
        for slot in (0, 1):
            change_row(jnp.clip(low + 2 * i - 2 + slot, low, high - 1), slot)
        for slot in (0, 1):
            add_up(jnp.minimum(low + 2 * i + slot, high - 1), slot)
        return carry

    def apply(j, carry):
        for d, (shift, variant, face) in enumerate(faces):
            u_ref[d, py, px, pz, at(j)] += delta_ref[d, at(j)]
            u_ref[(d,) + face + (at(j + shift),)] += delta_ref[3 + d, at(j)]
        u_ref[3, py, px, pz, at(j)] += delta_ref[6, at(j)]
        return carry

    lax.fori_loop(0, (high - low + 1) // 2 + 1, work, 0)
    lax.fori_loop(low, high, apply, 0)


def group_bounds(order_ref, group):
    spoiled = 0
    for n in range(COLOURS // 2, COLOURS):
        spoiled = spoiled + order_ref[n] // 2 % 2
    cut = jnp.where(spoiled == 0, 13, 12)
    return ((0, 4), (4, 8), (8, cut), (cut, SWEEPS * COLOURS))[group]


def run_sweeps(group, order_ref, u_ref, c_refs, d_ref, f_ref, delta_ref, sums_ref, rows):
    first, end = group_bounds(order_ref, group)
    last = int(group == 3)

    def one(n, carry):
        colour = order_ref[n % COLOURS]
        later = end - 1 - n
        for k in range(COLOURS):
            ky = k // 2 % 2

            @pl.when(colour == k)
            def _(k=k, ky=ky):
                low = jnp.maximum(Y_ROWS - 1 - later + (1 - ky) * (1 - last), 1 - ky)
                high = jnp.minimum(Y_ROWS + rows + later + last, 2 * Y_ROWS + rows - 1)
                sweep_colour(k, u_ref, c_refs, d_ref, f_ref, delta_ref, sums_ref, low, high)

        return carry

    lax.fori_loop(first, end, one, 0)


def write_strips(u_ref, up_ref, down_ref, rows):
    def strip(j, carry):
        for py, px, pz in PARITIES:
            for f in range(4):
                down_ref[f, py, j, px, pz] = u_ref[f, py, px, pz, at(Y_ROWS + j)]
                up_ref[f, py, j, px, pz] = u_ref[f, py, px, pz, at(rows + j)]
        return carry

    lax.fori_loop(0, Y_ROWS, strip, 0)


def load_margins(below_ref, above_ref, u_ref, rows):
    fields = tuple((f, f) for f in range(4))
    place_rows(below_ref, u_ref, fields, 0, Y_ROWS)
    place_rows(above_ref, u_ref, fields, Y_ROWS + rows, Y_ROWS)


def first_kernel(order_ref, own_ref, below_ref, above_ref, *refs):
    c_refs = refs[:8]
    d_ref, f_ref, u_ref, up_ref, down_ref, delta_ref, sums_ref = refs[8:]
    rows = own_ref.shape[2]
    place_rows(own_ref, u_ref, tuple((f, f) for f in range(4)), Y_ROWS, rows)
    load_margins(below_ref, above_ref, u_ref, rows)
    run_sweeps(0, order_ref, u_ref, c_refs, d_ref, f_ref, delta_ref, sums_ref, rows)
    write_strips(u_ref, up_ref, down_ref, rows)


def sweep_kernel(group, order_ref, old_ref, below_ref, above_ref, *refs):
    c_refs = refs[:8]
    d_ref, f_ref, u_ref, up_ref, down_ref, delta_ref, sums_ref = refs[8:]
    rows = u_ref.shape[-2] // SUBLANES - 2 * Y_ROWS
    load_margins(below_ref, above_ref, u_ref, rows)
    run_sweeps(group, order_ref, u_ref, c_refs, d_ref, f_ref, delta_ref, sums_ref, rows)
    write_strips(u_ref, up_ref, down_ref, rows)


def pair_sum(value, axis, reach):
    size = value.shape[axis]
    number = lax.broadcasted_iota(jnp.int32, value.shape, axis)
    low = (number // reach) % 2 == 0
    partner = jnp.where(low, pltpu.roll(value, size - reach, axis), pltpu.roll(value, reach, axis))
    return value + partner


def coarse_sum(value):
    return pair_sum(pair_sum(pair_sum(value, 1, 2), 0, 1), 0, 2)


def cycle_weights(cells):
    rate = 4.0 / cells
    screening = 2.0 * math.cosh(rate) - 2.0
    factor = screening / (2.0 * math.sinh(rate) * math.sinh(rate * cells / 2.0))
    return [factor * math.cosh(rate * (cells / 2.0 - k)) for k in range(cells)]


def final_kernel(order_ref, old_ref, below_ref, above_ref, *refs):
    c_refs = refs[:8]
    d_ref, f_ref, vs_ref, u_ref, out_ref, delta_ref, sums_ref, sum_ref = refs[8:]
    rows = u_ref.shape[-2] // SUBLANES - 2 * Y_ROWS
    load_margins(below_ref, above_ref, u_ref, rows)
    run_sweeps(3, order_ref, u_ref, c_refs, d_ref, f_ref, delta_ref, sums_ref, rows)
    sum_ref[...] = jnp.zeros(sum_ref.shape, jnp.float32)

    def residual(j, carry):
        y = j // 2
        for parity in PARITIES:
            found = partial_momentum(u_ref, c_refs, d_ref, f_ref, parity, (0, 1, 2), Y_ROWS + j)
            for d in range(3):
                sum_ref[d, y] = sum_ref[d, y] + gathered(found[d], parity)
        return carry

    lax.fori_loop(0, rows, residual, 0)
    sublanes = SUBLANES
    cells = 2 * sublanes // 4
    weights = cycle_weights(cells)
    number = lax.broadcasted_iota(jnp.int32, (SUBLANES, LANES), 0)
    for y in range(rows // 2):
        viscous = coarse_sum(vs_ref[y])
        viscous = jnp.where(viscous > 0, viscous, 1.0)
        for d in range(3):
            coarse = coarse_sum(sum_ref[d, y]) / viscous
            other = swapped(coarse)
            smooth = weights[0] * coarse + weights[cells // 2] * other
            for k in range(1, cells // 2):
                near = pltpu.roll(coarse, sublanes - 4 * k, 0)
                far = pltpu.roll(other, sublanes - 4 * k, 0)
                inside = number < sublanes - 4 * k
                smooth = smooth + weights[k] * jnp.where(inside, near, far)
                smooth = smooth + weights[k + cells // 2] * jnp.where(inside, far, near)
            sum_ref[d, y] = coarse_gain * smooth

    lane = lax.broadcasted_iota(jnp.int32, (SUBLANES, LANES), 1)
    width = LANES - 2 * Z_MARGIN
    spare = LANES - width

    def pack(j, carry):
        for py in (0, 1):
            for px in (0, 1):
                first, second = [], []
                for f in range(4):
                    even = u_ref[f, py, px, 0, at(Y_ROWS + j)]
                    odd = u_ref[f, py, px, 1, at(Y_ROWS + j)]
                    if f < 3:
                        added = sum_ref[f, j // 2]
                        even = even + added
                        odd = odd + added
                    low = even_lanes(even.shape)
                    first.append(jnp.where(low, even, pltpu.roll(odd, 1, 1)))
                    second.append(jnp.where(low, pltpu.roll(even, LANES - 1, 1), odd))
                for f in range(3):
                    for half, pieces in ((0, first), (2, second)):
                        own = pltpu.roll(pieces[f], LANES - Z_MARGIN, 1)
                        third = pltpu.roll(pieces[3], (width - Z_MARGIN - spare * f) % LANES, 1)
                        tile = jnp.where(lane < width, own, third)
                        for t in (0, 1):
                            out_ref[t + half, f, py, j, px] = tile[8 * t : 8 * t + 8]
        return carry

    lax.fori_loop(0, rows, pack, 0)


def refresh_pack_kernel(u_ref, left_ref, right_ref):
    rows = u_ref.shape[-2] // SUBLANES - 2 * Y_ROWS
    place = lax.broadcasted_iota(jnp.int32, (SUBLANES, LANES), 1) // Z_MARGIN

    def one(j, carry):
        for py in (0, 1):
            for px in (0, 1):
                to_left = jnp.zeros((SUBLANES, LANES), jnp.float32)
                to_right = to_left
                for f in range(4):
                    for pz in (0, 1):
                        slot = 2 * f + pz
                        value = u_ref[f, py, px, pz, at(Y_ROWS + j)]
                        shift = Z_MARGIN * slot
                        to_left = jnp.where(place == slot, pltpu.roll(value, (shift - Z_MARGIN) % LANES, 1), to_left)
                        to_right = jnp.where(
                            place == slot, pltpu.roll(value, (shift - LANES + 2 * Z_MARGIN) % LANES, 1), to_right
                        )
                left_ref[py, j, px] = to_left
                right_ref[py, j, px] = to_right
        return carry

    lax.fori_loop(0, rows, one, 0)


def refresh_kernel(old_ref, from_left_ref, from_right_ref, u_ref, up_ref, down_ref):
    rows = u_ref.shape[-2] // SUBLANES - 2 * Y_ROWS
    lane = lax.broadcasted_iota(jnp.int32, (SUBLANES, LANES), 1)

    def one(j, carry):
        for py in (0, 1):
            for px in (0, 1):
                low = from_left_ref[py, j, px]
                high = from_right_ref[py, j, px]
                for f in range(4):
                    for pz in (0, 1):
                        shift = Z_MARGIN * (2 * f + pz)
                        value = u_ref[f, py, px, pz, at(Y_ROWS + j)]
                        value = jnp.where(lane < Z_MARGIN, pltpu.roll(low, (-shift) % LANES, 1), value)
                        value = jnp.where(
                            lane >= LANES - Z_MARGIN, pltpu.roll(high, (-Z_MARGIN - shift) % LANES, 1), value
                        )
                        u_ref[f, py, px, pz, at(Y_ROWS + j)] = value
        return carry

    lax.fori_loop(0, rows, one, 0)
    write_strips(u_ref, up_ref, down_ref, rows)


def cut_windows(pieces, out_ref, place, parts):
    shape = pieces[0].shape
    tiles = len(pieces)
    width = tiles * LANES // parts
    lane = lax.broadcasted_iota(jnp.int32, shape, 1)
    for s in range(parts):
        start = width * s - Z_MARGIN
        first, offset = start // LANES, start % LANES
        found = jnp.zeros(shape, jnp.float32)
        if 0 <= first < tiles:
            found = jnp.where(lane < LANES - offset, pltpu.roll(pieces[first], (-offset) % LANES, 1), found)
        if 0 <= first + 1 < tiles:
            found = jnp.where(lane >= LANES - offset, pltpu.roll(pieces[first + 1], (-offset) % LANES, 1), found)
        out_ref[(s,) + place] = found


def pack_kernel(velocity_ref, pressure_ref, viscosity_ref, force_ref, state_ref, fixed_ref, row_ref):
    parts = state_ref.shape[0]
    half = state_ref.shape[5]
    tiles = row_ref.shape[2]
    for py in (0, 1):
        for t in range(tiles):
            columns = slice(LANES * t, LANES * (t + 1))
            viscous = viscosity_ref[py, :, columns]
            row_ref[py, 7, t] = viscous
            row_ref[py, 3, t] = viscous * pressure_ref[py, :, columns]
            for d in range(3):
                row_ref[py, d, t] = velocity_ref[d, py, :, columns]
                row_ref[py, 4 + d, t] = force_ref[d, py, :, columns]
    for py in (0, 1):
        for px in (0, 1):
            for f in range(8):
                pieces = [row_ref[py, f, t, pl.ds(px, half, stride=2), :] for t in range(tiles)]
                cut_windows(pieces, state_ref if f < 4 else fixed_ref, (f % 4, py, 0, px), parts)


def unpack_kernel(back_ref, viscosity_ref, velocity_ref, pressure_ref, row_ref):
    parts = back_ref.shape[0]
    tiles = row_ref.shape[2]
    width = tiles * LANES // parts
    spare = LANES - width
    shape = back_ref.shape[-2:]
    lane = lax.broadcasted_iota(jnp.int32, shape, 1)
    for py in (0, 1):
        for px in (0, 1):
            pieces = [[jnp.zeros(shape, jnp.float32)] * tiles for f in range(4)]
            for s in range(parts):
                got = [back_ref[s, f, py, 0, px] for f in range(3)]
                pressure = jnp.zeros(shape, jnp.float32)
                for f in range(3):
                    third = pltpu.roll(got[f], (spare * f - width) % LANES, 1)
                    pressure = jnp.where(lane // spare == f, third, pressure)
                for f, found in enumerate(got + [pressure]):
                    found = pltpu.roll(found, width * s % LANES, 1)
                    for t in range(tiles):
                        low = max(width * s - LANES * t, 0)
                        high = min(width * (s + 1) - LANES * t, LANES)
                        if low < high:
                            pieces[f][t] = jnp.where((lane >= low) & (lane < high), found, pieces[f][t])
            for f in range(4):
                for t in range(tiles):
                    row_ref[py, f, t, pl.ds(px, shape[0], stride=2), :] = pieces[f][t]
    for py in (0, 1):
        for t in range(tiles):
            columns = slice(LANES * t, LANES * (t + 1))
            for d in range(3):
                velocity_ref[d, py, :, columns] = row_ref[py, d, t]
            pressure_ref[py, :, columns] = row_ref[py, 3, t] / viscosity_ref[py, :, columns]


def shaped(*shape):
    return jax.ShapeDtypeStruct(shape, jnp.float32)


def kept(*shape):
    return pltpu.VMEM(shape, jnp.float32)


def hold(value):
    return pltpu.with_memory_space_constraint(value, pltpu.VMEM)


def params(mib):
    return pltpu.CompilerParams(vmem_limit_bytes=mib * 2**20)


def exchange(value_up, value_down, axis, count):
    below = lax.ppermute(value_up, axis, [(i, i + 1) for i in range(count - 1)])
    above = lax.ppermute(value_down, axis, [(i + 1, i) for i in range(count - 1)])
    return below, above


def body_windows(velocity, pressure_in, viscosity, body_force, colour_order):
    lon_cells, lat_cells, rad_cells = viscosity.shape
    parts = lax.axis_size("lon")
    lats = lax.axis_size("lat")
    rows = lat_cells // 2
    total = rows + 2 * Y_ROWS
    tile = (SUBLANES, LANES)
    own = shaped(4, 2, rows, 2, 2, *tile)
    strip = shaped(4, 2, Y_ROWS, 2, 2, *tile)
    sent = shaped(parts, 4, 2, rows, 2, lon_cells // 2, LANES)
    sent_block = pl.BlockSpec((parts, 4, 2, 1, 2, lon_cells // 2, LANES), lambda j: (0, 0, 0, j, 0, 0, 0))
    state_sent, fixed_sent = pl.pallas_call(
        pack_kernel,
        out_shape=(sent, sent),
        grid=(rows,),
        in_specs=[
            pl.BlockSpec((3, 2, lon_cells, rad_cells), lambda j: (0, j, 0, 0)),
            pl.BlockSpec((2, lon_cells, rad_cells), lambda j: (j, 0, 0)),
            pl.BlockSpec((2, lon_cells, rad_cells), lambda j: (j, 0, 0)),
            pl.BlockSpec((3, 2, lon_cells, rad_cells), lambda j: (0, j, 0, 0)),
        ],
        out_specs=(sent_block, sent_block),
        scratch_shapes=[pltpu.VMEM((2, 8, rad_cells // LANES, lon_cells, LANES), jnp.float32)],
        compiler_params=params(16),
    )(*[
        pltpu.with_memory_space_constraint(array, pltpu.HBM)
        for array in (
            velocity.transpose(0, 2, 1, 3), pressure_in.transpose(1, 0, 2),
            viscosity.transpose(1, 0, 2), body_force.transpose(0, 2, 1, 3),
        )
    ])

    def assembled(pieces):
        return pl.pallas_call(
            assemble_kernel,
            out_shape=(own, strip, strip),
            in_specs=[VMEM],
            out_specs=(VMEM, VMEM, VMEM),
            compiler_params=params(12),
        )(lax.all_to_all(pieces, "lon", 0, 0, tiled=True))

    own_fixed, fixed_up, fixed_down = assembled(fixed_sent)
    fixed_up, fixed_down, state_sent = lax.optimization_barrier((fixed_up, fixed_down, state_sent))
    fixed_below, fixed_above = exchange(fixed_up, fixed_down, "lat", lats)
    own_state, state_up, state_down = assembled(state_sent)
    below, above = exchange(state_up, state_down, "lat", lats)
    stacked = (2, 2, 2)
    *couplings, diagonals, force, viscous_sum = pl.pallas_call(
        coupling_kernel,
        out_shape=(
            *[kept(len(OFFSETS), pitch(total), LANES)] * 8,
            kept(3, *stacked, pitch(total), LANES),
            kept(3, *stacked, pitch(total), LANES),
            shaped(rows // 2, *tile),
        ),
        in_specs=[VMEM, VMEM, VMEM],
        out_specs=(VMEM,) * 11,
        scratch_shapes=[pltpu.VMEM((1,) + stacked + (pitch(total + 2), LANES), jnp.float32)],
        compiler_params=params(10),
    )(own_fixed, fixed_below, fixed_above)
    constants = [hold(array) for array in (*couplings, diagonals, force)]
    state_type = kept(4, *stacked, pitch(total), LANES)
    scratch = [
        pltpu.VMEM((7, pitch(total), LANES), jnp.float32),
        pltpu.VMEM((2, 6, 4) + tile, jnp.float32),
    ]
    state, up, down = pl.pallas_call(
        first_kernel,
        out_shape=(state_type, strip, strip),
        in_specs=[SMEM] + [VMEM] * 13,
        out_specs=(VMEM, VMEM, VMEM),
        scratch_shapes=scratch,
        compiler_params=params(8),
    )(colour_order, own_state, below, above, *constants)
    for g in (1, 2):
        below, above = exchange(up, down, "lat", lats)
        state, up, down = pl.pallas_call(
            functools.partial(sweep_kernel, g),
            out_shape=(state_type, strip, strip),
            in_specs=[SMEM] + [VMEM] * 13,
            out_specs=(VMEM, VMEM, VMEM),
            scratch_shapes=scratch,
            input_output_aliases={1: 0},
            compiler_params=params(8),
        )(colour_order, hold(state), below, above, *constants)
        if g == 1:
            packed = shaped(2, rows, 2, *tile)
            to_left, to_right = pl.pallas_call(
                refresh_pack_kernel,
                out_shape=(packed, packed),
                in_specs=[VMEM],
                out_specs=(VMEM, VMEM),
                compiler_params=params(6),
            )(hold(state))
            from_left, from_right = exchange(to_right, to_left, "lon", parts)
            state, up, down = pl.pallas_call(
                refresh_kernel,
                out_shape=(state_type, strip, strip),
                in_specs=[VMEM] * 3,
                out_specs=(VMEM, VMEM, VMEM),
                input_output_aliases={0: 0},
                compiler_params=params(6),
            )(hold(state), from_left, from_right)
    below, above = exchange(up, down, "lat", lats)
    state, packed = pl.pallas_call(
        final_kernel,
        out_shape=(state_type, shaped(parts, 3, 2, rows, 2, lon_cells // 2, LANES)),
        in_specs=[SMEM] + [VMEM] * 14,
        out_specs=(VMEM, VMEM),
        scratch_shapes=scratch + [pltpu.VMEM((3, rows // 2) + tile, jnp.float32)],
        input_output_aliases={1: 0},
        compiler_params=params(8),
    )(colour_order, hold(state), below, above, *constants, viscous_sum)
    back = lax.all_to_all(packed, "lon", 0, 0, tiled=True)
    velocity_out, pressure_out = pl.pallas_call(
        unpack_kernel,
        out_shape=(shaped(3, lat_cells, lon_cells, rad_cells), shaped(lat_cells, lon_cells, rad_cells)),
        grid=(rows,),
        in_specs=[
            pl.BlockSpec((parts, 3, 2, 1, 2, lon_cells // 2, LANES), lambda j: (0, 0, 0, j, 0, 0, 0)),
            pl.BlockSpec((2, lon_cells, rad_cells), lambda j: (j, 0, 0)),
        ],
        out_specs=(
            pl.BlockSpec((3, 2, lon_cells, rad_cells), lambda j: (0, j, 0, 0)),
            pl.BlockSpec((2, lon_cells, rad_cells), lambda j: (j, 0, 0)),
        ),
        scratch_shapes=[pltpu.VMEM((2, 4, rad_cells // LANES, lon_cells, LANES), jnp.float32)],
        compiler_params=params(16),
    )(back, viscosity.transpose(1, 0, 2))
    return velocity_out.transpose(0, 2, 1, 3), pressure_out.transpose(1, 0, 2)


unit_steps = ((1, 0, 0), (0, 1, 0), (0, 0, 1))


def extended_2(block, sides, width, periodic):
    for axis, dim in sides:
        count = lax.axis_size(axis)
        forward = [(i, i + 1) for i in range(count - 1)]
        if periodic:
            forward.append((count - 1, 0))
        backward = [(target, source) for source, target in forward]
        low = lax.ppermute(
            lax.slice_in_dim(block, block.shape[dim] - width, None, axis=dim), axis, forward
        )
        high = lax.ppermute(lax.slice_in_dim(block, 0, width, axis=dim), axis, backward)
        block = jnp.concatenate([low, block, high], axis=dim)
    return block


def stencil_offsets():
    result = []
    for step_x in (-1, 0, 1):
        for step_y in (-1, 0, 1):
            for step_z in (-1, 0, 1):
                reach = abs(step_x) + abs(step_y) + abs(step_z)
                if reach > 0:
                    result.append((step_x, step_y, step_z, 0.5 ** (reach - 1)))
    return result


def slide(values, offset, axis_no):
    if offset == 0:
        return values
    extent = values.shape[axis_no]
    padding = [(0, 0)] * values.ndim
    if offset > 0:
        padding[axis_no] = (0, offset)
        return lax.slice_in_dim(jnp.pad(values, padding), offset, offset + extent, axis=axis_no)
    padding[axis_no] = (-offset, 0)
    return lax.slice_in_dim(jnp.pad(values, padding), 0, extent, axis=axis_no)


def moved(values, step_x, step_y, step_z):
    base = values.ndim - 3
    result = slide(values, step_x, base)
    result = slide(result, step_y, base + 1)
    return slide(result, step_z, base + 2)


def blend(own_value, next_value):
    return 2.0 * own_value * next_value / jnp.maximum(own_value + next_value, 1.0)


def viscous_diagonal(viscous):
    running = jnp.zeros_like(viscous)
    for step_x, step_y, step_z, weight in stencil_offsets():
        running = running + weight * blend(viscous, moved(viscous, step_x, step_y, step_z))
    return running


def residuals(fields, viscous, diagonal, body_force):
    velocity = fields[:3]
    pressure = fields[3]
    applied = diagonal * velocity
    for step_x, step_y, step_z, weight in stencil_offsets():
        coupling = weight * blend(viscous, moved(viscous, step_x, step_y, step_z))
        applied = applied - coupling * moved(velocity, step_x, step_y, step_z)
    gradient = jnp.stack(
        [
            moved(pressure, -unit_step[0], -unit_step[1], -unit_step[2]) - pressure
            for unit_step in unit_steps
        ]
    )
    momentum = body_force - applied - gradient
    continuity = jnp.zeros_like(pressure)
    for axis_no, unit_step in enumerate(unit_steps):
        continuity = continuity - (
            moved(velocity[axis_no], unit_step[0], unit_step[1], unit_step[2]) - velocity[axis_no]
        )
    return (momentum, continuity)


def colour_step(fields, viscous, diagonal, inverse, weight_sum, body_force, chosen):
    momentum, continuity = residuals(fields, viscous, diagonal, body_force)
    scaled = momentum * inverse
    mismatch = -continuity
    for axis_no, unit_step in enumerate(unit_steps):
        mismatch = (
            mismatch
            + moved(scaled[axis_no], unit_step[0], unit_step[1], unit_step[2])
            - scaled[axis_no]
        )
    change = chosen * mismatch / weight_sum
    updates = []
    for axis_no, unit_step in enumerate(unit_steps):
        before = moved(chosen, -unit_step[0], -unit_step[1], -unit_step[2])
        earlier = moved(change, -unit_step[0], -unit_step[1], -unit_step[2])
        updates.append(inverse * ((chosen + before) * momentum[axis_no] + change - earlier))
    velocity = fields[:3] + damping * jnp.stack(updates)
    pressure = fields[3] + damping * change
    return jnp.concatenate([velocity, pressure[None]], axis=0)


def colour_codes(shape):
    lon_parity = jnp.arange(shape[0], dtype=jnp.int32) % 2
    lat_parity = jnp.arange(shape[1], dtype=jnp.int32) % 2
    rad_parity = jnp.arange(shape[2], dtype=jnp.int32) % 2
    return lon_parity[:, None, None] + 2 * lat_parity[None, :, None] + 4 * rad_parity[None, None, :]


def extend(fields, margin):
    beside_all = extended_2(fields, (("lon", 1),), margin, True)
    return extended_2(beside_all, (("lat", 2),), margin, False)


def cycle_kernel(distance, cycle_cells):
    decay_rate = 4.0 / cycle_cells
    screening = 2.0 * math.cosh(decay_rate) - 2.0
    factor = screening / (2.0 * math.sinh(decay_rate) * math.sinh(decay_rate * cycle_cells / 2.0))
    wrapped = jnp.mod(distance, cycle_cells).astype(jnp.float32)
    return factor * jnp.cosh(decay_rate * (cycle_cells / 2.0 - wrapped))


def body_general(velocity, pressure_in, viscosity, body_force, colour_order):
    groups = 1
    margin = 2 * groups
    lon_cells, lat_cells, rad_cells = viscosity.shape
    lat_total = lax.axis_size("lat") * lat_cells
    lat_global = (
        lax.axis_index("lat") * lat_cells
        - margin
        + jnp.arange(lat_cells + 2 * margin, dtype=jnp.int32)
    )
    inside_lat = ((lat_global >= 0) & (lat_global < lat_total)).astype(jnp.float32)
    inside = jnp.broadcast_to(
        inside_lat[None, :, None], (lon_cells + 2 * margin, lat_cells + 2 * margin, rad_cells)
    )
    constant_fields = jnp.concatenate([body_force, viscosity[None]], axis=0)
    constant_wide = extended_2(constant_fields, (("lon", 1), ("lat", 2)), margin, True) * inside
    force_wide = constant_wide[:3]
    viscous_wide = constant_wide[3]
    diagonal = viscous_diagonal(viscous_wide)
    inverse = jnp.where(inside > 0, 1.0 / jnp.where(diagonal > 0, diagonal, 1.0), 0.0)
    weight_raw = 3.0 * inverse
    for unit_step in unit_steps:
        weight_raw = weight_raw + moved(inverse, unit_step[0], unit_step[1], unit_step[2])
    weight_sum = jnp.where(weight_raw > 0, weight_raw, 1.0)
    parity_code = colour_codes(inside.shape)
    fields = jnp.concatenate([velocity, (pressure_in * viscosity)[None]], axis=0)

    def sweep_block(block_no, current):
        extended = extend(current, margin)
        colour = colour_order[(block_no * groups + 0) % COLOURS]
        chosen = (parity_code == colour).astype(jnp.float32) * inside
        extended = colour_step(
            extended, viscous_wide, diagonal, inverse, weight_sum, force_wide, chosen
        )
        return extended[:, margin : margin + lon_cells, margin : margin + lat_cells, :]

    fields = lax.fori_loop(0, SWEEPS * COLOURS // groups, sweep_block, fields)
    extended = extend(fields, margin)
    momentum, continuity = residuals(extended, viscous_wide, diagonal, force_wide)
    momentum = momentum[:, margin : margin + lon_cells, margin : margin + lat_cells, :]
    lon_coarse = lon_cells // 8
    lat_coarse = lat_cells // 4
    rad_coarse = rad_cells // 4
    cycle_cells = lax.axis_size("lon") * lon_coarse
    own_first = lax.axis_index("lon") * lon_coarse
    summed = momentum.reshape(3, lon_coarse, 8, lat_coarse, 4, rad_coarse, 4).sum(axis=(2, 4, 6))
    viscous_sum = viscosity.reshape(lon_coarse, 8, lat_coarse, 4, rad_coarse, 4).sum(axis=(1, 3, 5))
    coarse = jnp.transpose(summed / viscous_sum[None], (1, 0, 2, 3))
    shard_piece = lax.all_gather(coarse, "lon", axis=0, tiled=True)
    sources = jnp.arange(shard_piece.shape[0], dtype=jnp.int32)
    targets = own_first + jnp.arange(lon_coarse, dtype=jnp.int32)
    kernel_table = cycle_kernel(targets[None, :] - sources[:, None], cycle_cells)
    smooth = jnp.einsum("jcyz,ji->icyz", shard_piece, kernel_table, precision=lax.Precision.HIGHEST)
    smooth = jnp.transpose(smooth, (1, 0, 2, 3))
    spread = jnp.repeat(jnp.repeat(jnp.repeat(smooth, 8, axis=1), 4, axis=2), 4, axis=3)
    velocity_out = fields[:3] + coarse_gain * spread
    pressure_out = fields[3] / viscosity
    return (velocity_out, pressure_out)


def body(velocity, pressure_in, viscosity, body_force, colour_order):
    lon_cells, lat_cells, rad_cells = viscosity.shape
    parts = lax.axis_size("lon")
    fits = (
        parts == 4
        and parts * lon_cells == 4 * SUBLANES
        and lat_cells % 4 == 0
        and lat_cells >= 2 * Y_ROWS
        and rad_cells % LANES == 0
        and rad_cells // parts + 2 * Z_MARGIN == LANES
    )
    chosen = body_windows if fits else body_general
    return chosen(velocity, pressure_in, viscosity, body_force, colour_order)


def solution(mesh):
    placed = (
        P(None, "lon", "lat", None),
        P("lon", "lat", None),
        P("lon", "lat", None),
        P(None, "lon", "lat", None),
        P(),
    )
    return jax.shard_map(
        body,
        mesh=mesh,
        in_specs=placed,
        out_specs=(P(None, "lon", "lat", None), P("lon", "lat", None)),
        check_vma=False,
    )
```

```python
import functools
import math

import jax
import jax.numpy as jnp
from jax import lax
from jax.experimental import pallas as pl
from jax.experimental.pallas import tpu as pltpu
from jax.sharding import PartitionSpec as P

SWEEPS = 2
COLOURS = 8
damping = 0.6
coarse_gain = 0.25

LANES = 128
SUBLANES = 16
Z_MARGIN = 16
Y_ROWS = 4
PARITIES = [(py, px, pz) for py in (0, 1) for px in (0, 1) for pz in (0, 1)]
OFFSETS = [
    (oy, ox, oz, 0.5 ** (abs(oy) + abs(ox) + abs(oz) - 1))
    for oy in (-1, 0, 1)
    for ox in (-1, 0, 1)
    for oz in (-1, 0, 1)
    if (oy, ox, oz) != (0, 0, 0)
]
STEPS = ((0, 1, 0), (1, 0, 0), (0, 0, 1))
VMEM = pl.BlockSpec(memory_space=pltpu.VMEM)
SMEM = pl.BlockSpec(memory_space=pltpu.SMEM)


def neighbour(parity, offset):
    py, px, pz = parity
    oy, ox, oz = offset[:3]
    shift = -1 if (py == 0 and oy == -1) else 1 if (py == 1 and oy == 1) else 0
    x_moved = (px == 0 and ox == -1) or (px == 1 and ox == 1)
    z_moved = (pz == 0 and oz == -1) or (pz == 1 and oz == 1)
    return shift, int(x_moved) + 2 * int(z_moved), (py ^ (oy & 1), px ^ (ox & 1), pz ^ (oz & 1))


def even_lanes(shape):
    return lax.broadcasted_iota(jnp.int32, shape, len(shape) - 1) % 2 == 0


def swapped(value):
    return jnp.where(even_lanes(value.shape), pltpu.roll(value, LANES - 1, 1), pltpu.roll(value, 1, 1))


def moved_x(value, px):
    rows = value.shape[0]
    number = lax.broadcasted_iota(jnp.int32, value.shape, 0)
    if px == 0:
        turned = pltpu.roll(value, rows - 1, 0)
        edge = number == rows - 1
    else:
        turned = pltpu.roll(value, 1, 0)
        edge = number == 0
    return jnp.where(edge, swapped(turned), turned)


def moved_z(value, pz):
    return pltpu.roll(value, LANES - 2 if pz == 0 else 2, 1)


def at(j):
    return pl.ds(pl.multiple_of(j * SUBLANES, SUBLANES), SUBLANES)


def pitch(rows):
    return rows * SUBLANES + 8


def gathered(sums, parity):
    py, px, pz = parity
    along_x = sums[1] + moved_z(sums[3], 1 - pz)
    return sums[0] + moved_x(along_x, 1 - px) + moved_z(sums[2], 1 - pz)


def assemble_kernel(in_ref, own_ref, up_ref, down_ref, done_ref):
    fields, rows = own_ref.shape[0], own_ref.shape[2]
    done_ref[...] = jnp.zeros(done_ref.shape, jnp.float32)

    def one(j, carry):
        for f in range(fields):
            for py in (0, 1):
                for px in (0, 1):
                    for t in (0, 1):
                        a = in_ref[t, f, py, j, px]
                        b = in_ref[t + 2, f, py, j, px]
                        low = even_lanes(a.shape)
                        even = jnp.where(low, a, pltpu.roll(b, 1, 1))
                        odd = jnp.where(low, pltpu.roll(a, LANES - 1, 1), b)
                        own_ref[f, py, j, px, 0, 8 * t : 8 * t + 8] = even
                        own_ref[f, py, j, px, 1, 8 * t : 8 * t + 8] = odd
        return carry

    lax.fori_loop(0, rows, one, 0)
    for f in range(fields):
        for py in (0, 1):
            down_ref[f, py] = own_ref[f, py, 0:Y_ROWS]
            up_ref[f, py] = own_ref[f, py, rows - Y_ROWS : rows]


def place_rows(source, target_ref, fields, first, count):
    def one(j, carry):
        for py, px, pz in PARITIES:
            for f, g in fields:
                target_ref[g, py, px, pz, at(first + j)] = source[f, py, j, px, pz]
        return carry

    lax.fori_loop(0, count, one, 0)


def coupling_kernel(own_ref, below_ref, above_ref, *refs):
    c_refs = refs[:8]
    d_ref, f_ref, vs_ref, v_ref = refs[8:]
    rows = own_ref.shape[2]
    total = rows + 2 * Y_ROWS
    zero = jnp.zeros(own_ref.shape[-2:], jnp.float32)
    for py, px, pz in PARITIES:
        v_ref[0, py, px, pz, at(0)] = zero
        v_ref[0, py, px, pz, at(total + 1)] = zero
    for source, first, count in (
        (below_ref, 0, Y_ROWS), (own_ref, Y_ROWS, rows), (above_ref, Y_ROWS + rows, Y_ROWS)
    ):
        place_rows(source, f_ref, ((0, 0), (1, 1), (2, 2)), first, count)
        place_rows(source, v_ref, ((3, 0),), first + 1, count)

    def couple(j, carry):
        for parity in PARITIES:
            py, px, pz = parity
            mine = v_ref[0, py, px, pz, at(j + 1)]
            along_z = moved_z(mine, pz)
            seen = [mine, moved_x(mine, px), along_z, moved_x(along_z, px)]
            sums = [zero] * 4
            for n, offset in enumerate(OFFSETS):
                shift, variant, (ny, nx, nz) = neighbour(parity, offset)
                other = v_ref[0, ny, nx, nz, at(j + 1 + shift)]
                value = (2.0 * offset[3]) * seen[variant] * other / jnp.maximum(seen[variant] + other, 1.0)
                c_refs[4 * py + 2 * px + pz][n, at(j)] = value
                sums[variant] = sums[variant] + value
            running = gathered(sums, parity)
            d_ref[0, py, px, pz, at(j)] = running
            positive = (running > 0) & (mine > 0)
            d_ref[1, py, px, pz, at(j)] = jnp.where(positive, 1.0 / jnp.where(positive, running, 1.0), 0.0)
        return carry

    lax.fori_loop(0, total, couple, 0)

    def weigh(j, carry):
        for parity in PARITIES:
            py, px, pz = parity
            raw = 3.0 * d_ref[1, py, px, pz, at(j)]
            for step in STEPS:
                shift, variant, (ny, nx, nz) = neighbour(parity, step)
                other = d_ref[1, ny, nx, nz, at(j + shift)]
                if variant == 1:
                    other = moved_x(other, nx)
                elif variant == 2:
                    other = moved_z(other, nz)
                raw = raw + other
            inside = (v_ref[0, py, px, pz, at(j + 1)] > 0) & (raw > 0)
            d_ref[2, py, px, pz, at(j)] = jnp.where(inside, 1.0 / jnp.where(inside, raw, 1.0), 0.0)
        return carry

    lax.fori_loop(0, total - 1, weigh, 0)
    for py, px, pz in PARITIES:
        d_ref[2, py, px, pz, at(total - 1)] = zero
    for y in range(rows // 2):
        running = zero
        for j in (2 * y, 2 * y + 1):
            for py, px, pz in PARITIES:
                running = running + own_ref[3, py, j, px, pz]
        vs_ref[y] = running


def partial_momentum(u_ref, c_refs, d_ref, f_ref, parity, components, j):
    py, px, pz = parity
    sums = []
    p_here = u_ref[3, py, px, pz, at(j)]
    diagonal = d_ref[0, py, px, pz, at(j)]
    for d in components:
        first = f_ref[d, py, px, pz, at(j)] + p_here - diagonal * u_ref[d, py, px, pz, at(j)]
        sums.append([first, None, None, None])
    for n, offset in enumerate(OFFSETS):
        shift, variant, (ny, nx, nz) = neighbour(parity, offset)
        weight = c_refs[4 * py + 2 * px + pz][n, at(j)]
        for i, d in enumerate(components):
            value = weight * u_ref[d, ny, nx, nz, at(j + shift)]
            if offset[:3] == tuple(-s for s in STEPS[d]):
                value = value - u_ref[3, ny, nx, nz, at(j + shift)]
            sums[i][variant] = value if sums[i][variant] is None else sums[i][variant] + value
    return sums


def sweep_colour(colour, u_ref, c_refs, d_ref, f_ref, delta_ref, sums_ref, low, high):
    parity = (colour // 2 % 2, colour % 2, colour // 4)
    py, px, pz = parity
    faces = [neighbour(parity, step) for step in STEPS]

    def add_up(j, slot):
        found = partial_momentum(u_ref, c_refs, d_ref, f_ref, parity, (0, 1, 2), j)
        for d, (shift, variant, face) in enumerate(faces):
            found += partial_momentum(u_ref, c_refs, d_ref, f_ref, face, (d,), j + shift)
        for i, sums in enumerate(found):
            for v in range(4):
                sums_ref[slot, i, v] = sums[v]

    def change_row(j, slot):
        here = [gathered([sums_ref[slot, d, v] for v in range(4)], parity) for d in range(3)]
        there = [gathered([sums_ref[slot, 3 + d, v] for v in range(4)], faces[d][2]) for d in range(3)]
        inverse = d_ref[1, py, px, pz, at(j)]
        inverse_there = []
        total = None
        for d, (shift, variant, face) in enumerate(faces):
            inverse_there.append(d_ref[(1,) + face + (at(j + shift),)])
            term = there[d] * inverse_there[d] + u_ref[(d,) + face + (at(j + shift),)]
            if variant == 1:
                term = moved_x(term, face[1])
            elif variant == 2:
                term = moved_z(term, face[2])
            term = term - here[d] * inverse - u_ref[d, py, px, pz, at(j)]
            total = term if total is None else total + term
        weight = d_ref[2, py, px, pz, at(j)]
        change = total * weight
        for d, (shift, variant, face) in enumerate(faces):
            delta_ref[d, at(j)] = damping * inverse * (here[d] + change)
            back = change
            if variant == 1:
                back = moved_x(change, px)
            elif variant == 2:
                back = moved_z(change, pz)
            own = there[d]
            if d == 1 and py == 1:
                own = jnp.where(weight > 0, own, 0.0)
            if d == 2 and pz == 1:
                own = jnp.where(moved_z(weight, pz) > 0, own, 0.0)
            delta_ref[3 + d, at(j)] = damping * inverse_there[d] * (own - back)
        delta_ref[6, at(j)] = damping * change

    def begin(i):
        for slot in (0, 1):
            add_up(jnp.minimum(low + 2 * i + slot, high - 1), slot)

    def finish(i):
        for slot in (0, 1):
            change_row(jnp.minimum(low + 2 * i + slot, high - 1), slot)

    def work(i, carry):
        finish(i - 1)
        begin(i)
        return carry

    def apply(j, carry):
        for d, (shift, variant, face) in enumerate(faces):
            u_ref[d, py, px, pz, at(j)] += delta_ref[d, at(j)]
            u_ref[(d,) + face + (at(j + shift),)] += delta_ref[3 + d, at(j)]
        u_ref[3, py, px, pz, at(j)] += delta_ref[6, at(j)]
        return carry

    pairs = (high - low + 1) // 2
    begin(0)
    lax.fori_loop(1, pairs, work, 0)
    finish(pairs - 1)
    lax.fori_loop(low, high, apply, 0)


def group_bounds(order_ref, group):
    spoiled = 0
    for n in range(COLOURS // 2, COLOURS):
        spoiled = spoiled + order_ref[n] // 2 % 2
    cut = jnp.where(spoiled == 0, 13, 12)
    return ((0, 4), (4, 8), (8, cut), (cut, SWEEPS * COLOURS))[group]


def run_sweeps(group, order_ref, u_ref, c_refs, d_ref, f_ref, delta_ref, sums_ref, rows):
    first, end = group_bounds(order_ref, group)
    last = int(group == 3)

    def one(n, carry):
        colour = order_ref[n % COLOURS]
        later = end - 1 - n
        for k in range(COLOURS):
            ky = k // 2 % 2

            @pl.when(colour == k)
            def _(k=k, ky=ky):
                low = jnp.maximum(Y_ROWS - 1 - later + (1 - ky) * (1 - last), 1 - ky)
                high = jnp.minimum(Y_ROWS + rows + later + last, 2 * Y_ROWS + rows - 1)
                sweep_colour(k, u_ref, c_refs, d_ref, f_ref, delta_ref, sums_ref, low, high)

        return carry

    lax.fori_loop(first, end, one, 0)


def write_strips(u_ref, up_ref, down_ref, rows):
    def strip(j, carry):
        for py, px, pz in PARITIES:
            for f in range(4):
                down_ref[f, py, j, px, pz] = u_ref[f, py, px, pz, at(Y_ROWS + j)]
                up_ref[f, py, j, px, pz] = u_ref[f, py, px, pz, at(rows + j)]
        return carry

    lax.fori_loop(0, Y_ROWS, strip, 0)


def load_margins(below_ref, above_ref, u_ref, rows):
    fields = tuple((f, f) for f in range(4))
    place_rows(below_ref, u_ref, fields, 0, Y_ROWS)
    place_rows(above_ref, u_ref, fields, Y_ROWS + rows, Y_ROWS)


def first_kernel(order_ref, own_ref, below_ref, above_ref, *refs):
    c_refs = refs[:8]
    d_ref, f_ref, u_ref, up_ref, down_ref, delta_ref, sums_ref = refs[8:]
    rows = own_ref.shape[2]
    place_rows(own_ref, u_ref, tuple((f, f) for f in range(4)), Y_ROWS, rows)
    load_margins(below_ref, above_ref, u_ref, rows)
    run_sweeps(0, order_ref, u_ref, c_refs, d_ref, f_ref, delta_ref, sums_ref, rows)
    write_strips(u_ref, up_ref, down_ref, rows)


def sweep_kernel(group, order_ref, old_ref, below_ref, above_ref, *refs):
    c_refs = refs[:8]
    d_ref, f_ref, u_ref, up_ref, down_ref, delta_ref, sums_ref = refs[8:]
    rows = u_ref.shape[-2] // SUBLANES - 2 * Y_ROWS
    load_margins(below_ref, above_ref, u_ref, rows)
    run_sweeps(group, order_ref, u_ref, c_refs, d_ref, f_ref, delta_ref, sums_ref, rows)
    write_strips(u_ref, up_ref, down_ref, rows)


def pair_sum(value, axis, reach):
    size = value.shape[axis]
    number = lax.broadcasted_iota(jnp.int32, value.shape, axis)
    low = (number // reach) % 2 == 0
    partner = jnp.where(low, pltpu.roll(value, size - reach, axis), pltpu.roll(value, reach, axis))
    return value + partner


def coarse_sum(value):
    return pair_sum(pair_sum(pair_sum(value, 1, 2), 0, 1), 0, 2)


def cycle_weights(cells):
    rate = 4.0 / cells
    screening = 2.0 * math.cosh(rate) - 2.0
    factor = screening / (2.0 * math.sinh(rate) * math.sinh(rate * cells / 2.0))
    return [factor * math.cosh(rate * (cells / 2.0 - k)) for k in range(cells)]


def final_kernel(order_ref, old_ref, below_ref, above_ref, *refs):
    c_refs = refs[:8]
    d_ref, f_ref, vs_ref, u_ref, out_ref, delta_ref, sums_ref, sum_ref, apart_ref = refs[8:]
    rows = u_ref.shape[-2] // SUBLANES - 2 * Y_ROWS
    load_margins(below_ref, above_ref, u_ref, rows)
    run_sweeps(3, order_ref, u_ref, c_refs, d_ref, f_ref, delta_ref, sums_ref, rows)
    apart_ref[...] = jnp.zeros(apart_ref.shape, jnp.float32)

    def residual(j, carry):
        y = j // 2
        apart = {}
        for parity in PARITIES:
            _, px, pz = parity
            found = partial_momentum(u_ref, c_refs, d_ref, f_ref, parity, (0, 1, 2), Y_ROWS + j)
            for d in range(3):
                for v, slot in enumerate((0, 1 + px, 3 + pz, 5 + 2 * px + pz)):
                    apart[d, slot] = found[d][v] + apart[d, slot] if (d, slot) in apart else found[d][v]
        for (d, slot), value in apart.items():
            apart_ref[d, y, slot] += value
        return carry

    lax.fori_loop(0, rows, residual, 0)
    for y in range(rows // 2):
        for d in range(3):
            total = apart_ref[d, y, 0]
            for px in (0, 1):
                along_x = apart_ref[d, y, 1 + px]
                for pz in (0, 1):
                    along_x = along_x + moved_z(apart_ref[d, y, 5 + 2 * px + pz], 1 - pz)
                total = total + moved_x(along_x, 1 - px)
            for pz in (0, 1):
                total = total + moved_z(apart_ref[d, y, 3 + pz], 1 - pz)
            sum_ref[d, y] = total
    sublanes = SUBLANES
    cells = 2 * sublanes // 4
    weights = cycle_weights(cells)
    number = lax.broadcasted_iota(jnp.int32, (SUBLANES, LANES), 0)
    for y in range(rows // 2):
        viscous = coarse_sum(vs_ref[y])
        viscous = jnp.where(viscous > 0, viscous, 1.0)
        for d in range(3):
            coarse = coarse_sum(sum_ref[d, y]) / viscous
            other = swapped(coarse)
            smooth = weights[0] * coarse + weights[cells // 2] * other
            for k in range(1, cells // 2):
                near = pltpu.roll(coarse, sublanes - 4 * k, 0)
                far = pltpu.roll(other, sublanes - 4 * k, 0)
                inside = number < sublanes - 4 * k
                smooth = smooth + weights[k] * jnp.where(inside, near, far)
                smooth = smooth + weights[k + cells // 2] * jnp.where(inside, far, near)
            sum_ref[d, y] = coarse_gain * smooth

    lane = lax.broadcasted_iota(jnp.int32, (SUBLANES, LANES), 1)
    width = LANES - 2 * Z_MARGIN
    spare = LANES - width

    def pack(j, carry):
        for py in (0, 1):
            for px in (0, 1):
                first, second = [], []
                for f in range(4):
                    even = u_ref[f, py, px, 0, at(Y_ROWS + j)]
                    odd = u_ref[f, py, px, 1, at(Y_ROWS + j)]
                    if f < 3:
                        added = sum_ref[f, j // 2]
                        even = even + added
                        odd = odd + added
                    low = even_lanes(even.shape)
                    first.append(jnp.where(low, even, pltpu.roll(odd, 1, 1)))
                    second.append(jnp.where(low, pltpu.roll(even, LANES - 1, 1), odd))
                for f in range(3):
                    for half, pieces in ((0, first), (2, second)):
                        own = pltpu.roll(pieces[f], LANES - Z_MARGIN, 1)
                        third = pltpu.roll(pieces[3], (width - Z_MARGIN - spare * f) % LANES, 1)
                        tile = jnp.where(lane < width, own, third)
                        for t in (0, 1):
                            out_ref[t + half, f, py, j, px] = tile[8 * t : 8 * t + 8]
        return carry

    lax.fori_loop(0, rows, pack, 0)


def refresh_pack_kernel(u_ref, left_ref, right_ref):
    rows = u_ref.shape[-2] // SUBLANES - 2 * Y_ROWS
    place = lax.broadcasted_iota(jnp.int32, (SUBLANES, LANES), 1) // Z_MARGIN

    def one(j, carry):
        for py in (0, 1):
            for px in (0, 1):
                to_left = jnp.zeros((SUBLANES, LANES), jnp.float32)
                to_right = to_left
                for f in range(4):
                    for pz in (0, 1):
                        slot = 2 * f + pz
                        value = u_ref[f, py, px, pz, at(Y_ROWS + j)]
                        shift = Z_MARGIN * slot
                        to_left = jnp.where(place == slot, pltpu.roll(value, (shift - Z_MARGIN) % LANES, 1), to_left)
                        to_right = jnp.where(
                            place == slot, pltpu.roll(value, (shift - LANES + 2 * Z_MARGIN) % LANES, 1), to_right
                        )
                left_ref[py, j, px] = to_left
                right_ref[py, j, px] = to_right
        return carry

    lax.fori_loop(0, rows, one, 0)


def refresh_kernel(old_ref, from_left_ref, from_right_ref, u_ref, up_ref, down_ref):
    rows = u_ref.shape[-2] // SUBLANES - 2 * Y_ROWS
    lane = lax.broadcasted_iota(jnp.int32, (SUBLANES, LANES), 1)

    def one(j, carry):
        for py in (0, 1):
            for px in (0, 1):
                low = from_left_ref[py, j, px]
                high = from_right_ref[py, j, px]
                for f in range(4):
                    for pz in (0, 1):
                        shift = Z_MARGIN * (2 * f + pz)
                        value = u_ref[f, py, px, pz, at(Y_ROWS + j)]
                        value = jnp.where(lane < Z_MARGIN, pltpu.roll(low, (-shift) % LANES, 1), value)
                        value = jnp.where(
                            lane >= LANES - Z_MARGIN, pltpu.roll(high, (-Z_MARGIN - shift) % LANES, 1), value
                        )
                        u_ref[f, py, px, pz, at(Y_ROWS + j)] = value
        return carry

    lax.fori_loop(0, rows, one, 0)
    write_strips(u_ref, up_ref, down_ref, rows)


def cut_windows(pieces, out_ref, place, parts):
    shape = pieces[0].shape
    tiles = len(pieces)
    width = tiles * LANES // parts
    lane = lax.broadcasted_iota(jnp.int32, shape, 1)
    for s in range(parts):
        start = width * s - Z_MARGIN
        first, offset = start // LANES, start % LANES
        found = jnp.zeros(shape, jnp.float32)
        if 0 <= first < tiles:
            found = jnp.where(lane < LANES - offset, pltpu.roll(pieces[first], (-offset) % LANES, 1), found)
        if 0 <= first + 1 < tiles:
            found = jnp.where(lane >= LANES - offset, pltpu.roll(pieces[first + 1], (-offset) % LANES, 1), found)
        out_ref[(s,) + place] = found


def write_windows(row_ref, out_ref, j):
    parts, fields = out_ref.shape[:2]
    half = out_ref.shape[5]
    for py in (0, 1):
        for px in (0, 1):
            for f in range(fields):
                pieces = [row_ref[py, f, t, pl.ds(px, half, stride=2), :] for t in range(row_ref.shape[2])]
                cut_windows(pieces, out_ref, (f, py, j, px), parts)


def pack_fixed_kernel(force_ref, viscosity_ref, out_ref, row_ref):
    def one(j, carry):
        for py in (0, 1):
            for t in range(row_ref.shape[2]):
                columns = slice(LANES * t, LANES * (t + 1))
                row_ref[py, 3, t] = viscosity_ref[2 * j + py, :, columns]
                for d in range(3):
                    row_ref[py, d, t] = force_ref[d, 2 * j + py, :, columns]
        write_windows(row_ref, out_ref, j)
        return carry

    lax.fori_loop(0, out_ref.shape[3], one, 0)


def pack_state_kernel(velocity_ref, viscosity_ref, pressure_ref, out_ref, row_ref):
    def one(j, carry):
        for py in (0, 1):
            for t in range(row_ref.shape[2]):
                columns = slice(LANES * t, LANES * (t + 1))
                row_ref[py, 3, t] = viscosity_ref[2 * j + py, :, columns] * pressure_ref[2 * j + py, :, columns]
                for d in range(3):
                    row_ref[py, d, t] = velocity_ref[d, 2 * j + py, :, columns]
        write_windows(row_ref, out_ref, j)
        return carry

    lax.fori_loop(0, out_ref.shape[3], one, 0)


def unpack_kernel(back_ref, viscosity_ref, velocity_ref, pressure_ref, row_ref):
    parts = back_ref.shape[0]
    tiles = row_ref.shape[2]
    width = tiles * LANES // parts
    spare = LANES - width
    shape = back_ref.shape[-2:]
    lane = lax.broadcasted_iota(jnp.int32, shape, 1)
    for py in (0, 1):
        for px in (0, 1):
            pieces = [[jnp.zeros(shape, jnp.float32)] * tiles for f in range(4)]
            for s in range(parts):
                got = [back_ref[s, f, py, 0, px] for f in range(3)]
                pressure = jnp.zeros(shape, jnp.float32)
                for f in range(3):
                    third = pltpu.roll(got[f], (spare * f - width) % LANES, 1)
                    pressure = jnp.where(lane // spare == f, third, pressure)
                for f, found in enumerate(got + [pressure]):
                    found = pltpu.roll(found, width * s % LANES, 1)
                    for t in range(tiles):
                        low = max(width * s - LANES * t, 0)
                        high = min(width * (s + 1) - LANES * t, LANES)
                        if low < high:
                            pieces[f][t] = jnp.where((lane >= low) & (lane < high), found, pieces[f][t])
            for f in range(4):
                for t in range(tiles):
                    row_ref[py, f, t, pl.ds(px, shape[0], stride=2), :] = pieces[f][t]
    for py in (0, 1):
        for t in range(tiles):
            columns = slice(LANES * t, LANES * (t + 1))
            for d in range(3):
                velocity_ref[d, py, :, columns] = row_ref[py, d, t]
            pressure_ref[py, :, columns] = row_ref[py, 3, t] / viscosity_ref[py, :, columns]


def shaped(*shape):
    return jax.ShapeDtypeStruct(shape, jnp.float32)


def kept(*shape):
    return pltpu.VMEM(shape, jnp.float32)


def hold(value):
    return pltpu.with_memory_space_constraint(value, pltpu.VMEM)


def params(mib):
    return pltpu.CompilerParams(vmem_limit_bytes=mib * 2**20)


def exchange(value_up, value_down, axis, count):
    below = lax.ppermute(value_up, axis, [(i, i + 1) for i in range(count - 1)])
    above = lax.ppermute(value_down, axis, [(i + 1, i) for i in range(count - 1)])
    return below, above


def body_windows(velocity, pressure_in, viscosity, body_force, colour_order):
    lon_cells, lat_cells, rad_cells = viscosity.shape
    parts = lax.axis_size("lon")
    lats = lax.axis_size("lat")
    rows = lat_cells // 2
    total = rows + 2 * Y_ROWS
    tile = (SUBLANES, LANES)
    strip = shaped(4, 2, Y_ROWS, 2, 2, *tile)
    steps = 2 - rows % 2
    several = pl.BlockSpec((3, lat_cells // steps, lon_cells, rad_cells), lambda j: (0, j, 0, 0))
    single = pl.BlockSpec((lat_cells // steps, lon_cells, rad_cells), lambda j: (j, 0, 0))

    def packed_windows(kernel, fields, specs, *arrays):
        return pl.pallas_call(
            kernel,
            out_shape=shaped(parts, fields, 2, rows, 2, lon_cells // 2, LANES),
            grid=(steps,),
            in_specs=specs,
            out_specs=pl.BlockSpec(
                (parts, fields, 2, rows // steps, 2, lon_cells // 2, LANES), lambda j: (0, 0, 0, j, 0, 0, 0)
            ),
            scratch_shapes=[pltpu.VMEM((2, fields, rad_cells // LANES, lon_cells, LANES), jnp.float32)],
            compiler_params=params(12),
        )(*[pltpu.with_memory_space_constraint(array, pltpu.HBM) for array in arrays])

    def assembled(pieces):
        fields = pieces.shape[1]
        strips = shaped(fields, 2, Y_ROWS, 2, 2, *tile)
        return pl.pallas_call(
            assemble_kernel,
            out_shape=(shaped(fields, 2, rows, 2, 2, *tile), strips, strips, shaped(8, LANES)),
            in_specs=[VMEM],
            out_specs=(VMEM, VMEM, VMEM, VMEM),
            compiler_params=params(14),
        )(lax.all_to_all(pieces, "lon", 0, 0, tiled=True))

    fixed_sent = packed_windows(
        pack_fixed_kernel, 4, [several, single],
        body_force.transpose(0, 2, 1, 3), viscosity.transpose(1, 0, 2),
    )
    state_sent = packed_windows(
        pack_state_kernel, 4, [several, single, single],
        velocity.transpose(0, 2, 1, 3), viscosity.transpose(1, 0, 2), pressure_in.transpose(1, 0, 2),
    )
    own_fixed, fixed_up, fixed_down, done = assembled(fixed_sent)
    done, state_sent = lax.optimization_barrier((done, state_sent))
    fixed_below, fixed_above = exchange(fixed_up, fixed_down, "lat", lats)
    own_state, up, down, done = assembled(state_sent)
    below, above = exchange(up, down, "lat", lats)
    stacked = (2, 2, 2)
    state_type = kept(4, *stacked, pitch(total), LANES)
    *couplings, diagonals, force, viscous_sum = pl.pallas_call(
        coupling_kernel,
        out_shape=(
            *[kept(len(OFFSETS), pitch(total), LANES)] * 8,
            kept(3, *stacked, pitch(total), LANES),
            kept(3, *stacked, pitch(total), LANES),
            shaped(rows // 2, *tile),
        ),
        in_specs=[VMEM, VMEM, VMEM],
        out_specs=(VMEM,) * 11,
        scratch_shapes=[pltpu.VMEM((1,) + stacked + (pitch(total + 2), LANES), jnp.float32)],
        compiler_params=params(10),
    )(own_fixed, fixed_below, fixed_above)
    constants = [hold(array) for array in (*couplings, diagonals, force)]
    scratch = [
        pltpu.VMEM((7, pitch(total), LANES), jnp.float32),
        pltpu.VMEM((2, 6, 4) + tile, jnp.float32),
    ]
    state, up, down = pl.pallas_call(
        first_kernel,
        out_shape=(state_type, strip, strip),
        in_specs=[SMEM] + [VMEM] * 13,
        out_specs=(VMEM, VMEM, VMEM),
        scratch_shapes=scratch,
        compiler_params=params(8),
    )(colour_order, own_state, below, above, *constants)
    for g in (1, 2):
        below, above = exchange(up, down, "lat", lats)
        state, up, down = pl.pallas_call(
            functools.partial(sweep_kernel, g),
            out_shape=(state_type, strip, strip),
            in_specs=[SMEM] + [VMEM] * 13,
            out_specs=(VMEM, VMEM, VMEM),
            scratch_shapes=scratch,
            input_output_aliases={1: 0},
            compiler_params=params(8),
        )(colour_order, hold(state), below, above, *constants)
        if g == 1:
            packed = shaped(2, rows, 2, *tile)
            to_left, to_right = pl.pallas_call(
                refresh_pack_kernel,
                out_shape=(packed, packed),
                in_specs=[VMEM],
                out_specs=(VMEM, VMEM),
                compiler_params=params(6),
            )(hold(state))
            from_left, from_right = exchange(to_right, to_left, "lon", parts)
            state, up, down = pl.pallas_call(
                refresh_kernel,
                out_shape=(state_type, strip, strip),
                in_specs=[VMEM] * 3,
                out_specs=(VMEM, VMEM, VMEM),
                input_output_aliases={0: 0},
                compiler_params=params(6),
            )(hold(state), from_left, from_right)
    below, above = exchange(up, down, "lat", lats)
    state, packed = pl.pallas_call(
        final_kernel,
        out_shape=(state_type, shaped(parts, 3, 2, rows, 2, lon_cells // 2, LANES)),
        in_specs=[SMEM] + [VMEM] * 14,
        out_specs=(VMEM, VMEM),
        scratch_shapes=scratch
        + [pltpu.VMEM((3, rows // 2) + tile, jnp.float32), pltpu.VMEM((3, rows // 2, 9) + tile, jnp.float32)],
        input_output_aliases={1: 0},
        compiler_params=params(8),
    )(colour_order, hold(state), below, above, *constants, viscous_sum)
    back = lax.all_to_all(packed, "lon", 0, 0, tiled=True)
    velocity_out, pressure_out = pl.pallas_call(
        unpack_kernel,
        out_shape=(shaped(3, lat_cells, lon_cells, rad_cells), shaped(lat_cells, lon_cells, rad_cells)),
        grid=(rows,),
        in_specs=[
            pl.BlockSpec((parts, 3, 2, 1, 2, lon_cells // 2, LANES), lambda j: (0, 0, 0, j, 0, 0, 0)),
            pl.BlockSpec((2, lon_cells, rad_cells), lambda j: (j, 0, 0)),
        ],
        out_specs=(
            pl.BlockSpec((3, 2, lon_cells, rad_cells), lambda j: (0, j, 0, 0)),
            pl.BlockSpec((2, lon_cells, rad_cells), lambda j: (j, 0, 0)),
        ),
        scratch_shapes=[pltpu.VMEM((2, 4, rad_cells // LANES, lon_cells, LANES), jnp.float32)],
        compiler_params=params(16),
    )(back, viscosity.transpose(1, 0, 2))
    return velocity_out.transpose(0, 2, 1, 3), pressure_out.transpose(1, 0, 2)


unit_steps = ((1, 0, 0), (0, 1, 0), (0, 0, 1))


def extended_2(block, sides, width, periodic):
    for axis, dim in sides:
        count = lax.axis_size(axis)
        forward = [(i, i + 1) for i in range(count - 1)]
        if periodic:
            forward.append((count - 1, 0))
        backward = [(target, source) for source, target in forward]
        low = lax.ppermute(
            lax.slice_in_dim(block, block.shape[dim] - width, None, axis=dim), axis, forward
        )
        high = lax.ppermute(lax.slice_in_dim(block, 0, width, axis=dim), axis, backward)
        block = jnp.concatenate([low, block, high], axis=dim)
    return block


def stencil_offsets():
    result = []
    for step_x in (-1, 0, 1):
        for step_y in (-1, 0, 1):
            for step_z in (-1, 0, 1):
                reach = abs(step_x) + abs(step_y) + abs(step_z)
                if reach > 0:
                    result.append((step_x, step_y, step_z, 0.5 ** (reach - 1)))
    return result


def slide(values, offset, axis_no):
    if offset == 0:
        return values
    extent = values.shape[axis_no]
    padding = [(0, 0)] * values.ndim
    if offset > 0:
        padding[axis_no] = (0, offset)
        return lax.slice_in_dim(jnp.pad(values, padding), offset, offset + extent, axis=axis_no)
    padding[axis_no] = (-offset, 0)
    return lax.slice_in_dim(jnp.pad(values, padding), 0, extent, axis=axis_no)


def moved(values, step_x, step_y, step_z):
    base = values.ndim - 3
    result = slide(values, step_x, base)
    result = slide(result, step_y, base + 1)
    return slide(result, step_z, base + 2)


def blend(own_value, next_value):
    return 2.0 * own_value * next_value / jnp.maximum(own_value + next_value, 1.0)


def viscous_diagonal(viscous):
    running = jnp.zeros_like(viscous)
    for step_x, step_y, step_z, weight in stencil_offsets():
        running = running + weight * blend(viscous, moved(viscous, step_x, step_y, step_z))
    return running


def residuals(fields, viscous, diagonal, body_force):
    velocity = fields[:3]
    pressure = fields[3]
    applied = diagonal * velocity
    for step_x, step_y, step_z, weight in stencil_offsets():
        coupling = weight * blend(viscous, moved(viscous, step_x, step_y, step_z))
        applied = applied - coupling * moved(velocity, step_x, step_y, step_z)
    gradient = jnp.stack(
        [
            moved(pressure, -unit_step[0], -unit_step[1], -unit_step[2]) - pressure
            for unit_step in unit_steps
        ]
    )
    momentum = body_force - applied - gradient
    continuity = jnp.zeros_like(pressure)
    for axis_no, unit_step in enumerate(unit_steps):
        continuity = continuity - (
            moved(velocity[axis_no], unit_step[0], unit_step[1], unit_step[2]) - velocity[axis_no]
        )
    return (momentum, continuity)


def colour_step(fields, viscous, diagonal, inverse, weight_sum, body_force, chosen):
    momentum, continuity = residuals(fields, viscous, diagonal, body_force)
    scaled = momentum * inverse
    mismatch = -continuity
    for axis_no, unit_step in enumerate(unit_steps):
        mismatch = (
            mismatch
            + moved(scaled[axis_no], unit_step[0], unit_step[1], unit_step[2])
            - scaled[axis_no]
        )
    change = chosen * mismatch / weight_sum
    updates = []
    for axis_no, unit_step in enumerate(unit_steps):
        before = moved(chosen, -unit_step[0], -unit_step[1], -unit_step[2])
        earlier = moved(change, -unit_step[0], -unit_step[1], -unit_step[2])
        updates.append(inverse * ((chosen + before) * momentum[axis_no] + change - earlier))
    velocity = fields[:3] + damping * jnp.stack(updates)
    pressure = fields[3] + damping * change
    return jnp.concatenate([velocity, pressure[None]], axis=0)


def colour_codes(shape):
    lon_parity = jnp.arange(shape[0], dtype=jnp.int32) % 2
    lat_parity = jnp.arange(shape[1], dtype=jnp.int32) % 2
    rad_parity = jnp.arange(shape[2], dtype=jnp.int32) % 2
    return lon_parity[:, None, None] + 2 * lat_parity[None, :, None] + 4 * rad_parity[None, None, :]


def extend(fields, margin):
    beside_all = extended_2(fields, (("lon", 1),), margin, True)
    return extended_2(beside_all, (("lat", 2),), margin, False)


def cycle_kernel(distance, cycle_cells):
    decay_rate = 4.0 / cycle_cells
    screening = 2.0 * math.cosh(decay_rate) - 2.0
    factor = screening / (2.0 * math.sinh(decay_rate) * math.sinh(decay_rate * cycle_cells / 2.0))
    wrapped = jnp.mod(distance, cycle_cells).astype(jnp.float32)
    return factor * jnp.cosh(decay_rate * (cycle_cells / 2.0 - wrapped))


def body_general(velocity, pressure_in, viscosity, body_force, colour_order):
    groups = 1
    margin = 2 * groups
    lon_cells, lat_cells, rad_cells = viscosity.shape
    lat_total = lax.axis_size("lat") * lat_cells
    lat_global = (
        lax.axis_index("lat") * lat_cells
        - margin
        + jnp.arange(lat_cells + 2 * margin, dtype=jnp.int32)
    )
    inside_lat = ((lat_global >= 0) & (lat_global < lat_total)).astype(jnp.float32)
    inside = jnp.broadcast_to(
        inside_lat[None, :, None], (lon_cells + 2 * margin, lat_cells + 2 * margin, rad_cells)
    )
    constant_fields = jnp.concatenate([body_force, viscosity[None]], axis=0)
    constant_wide = extended_2(constant_fields, (("lon", 1), ("lat", 2)), margin, True) * inside
    force_wide = constant_wide[:3]
    viscous_wide = constant_wide[3]
    diagonal = viscous_diagonal(viscous_wide)
    inverse = jnp.where(inside > 0, 1.0 / jnp.where(diagonal > 0, diagonal, 1.0), 0.0)
    weight_raw = 3.0 * inverse
    for unit_step in unit_steps:
        weight_raw = weight_raw + moved(inverse, unit_step[0], unit_step[1], unit_step[2])
    weight_sum = jnp.where(weight_raw > 0, weight_raw, 1.0)
    parity_code = colour_codes(inside.shape)
    fields = jnp.concatenate([velocity, (pressure_in * viscosity)[None]], axis=0)

    def sweep_block(block_no, current):
        extended = extend(current, margin)
        colour = colour_order[(block_no * groups + 0) % COLOURS]
        chosen = (parity_code == colour).astype(jnp.float32) * inside
        extended = colour_step(
            extended, viscous_wide, diagonal, inverse, weight_sum, force_wide, chosen
        )
        return extended[:, margin : margin + lon_cells, margin : margin + lat_cells, :]

    fields = lax.fori_loop(0, SWEEPS * COLOURS // groups, sweep_block, fields)
    extended = extend(fields, margin)
    momentum, continuity = residuals(extended, viscous_wide, diagonal, force_wide)
    momentum = momentum[:, margin : margin + lon_cells, margin : margin + lat_cells, :]
    lon_coarse = lon_cells // 8
    lat_coarse = lat_cells // 4
    rad_coarse = rad_cells // 4
    cycle_cells = lax.axis_size("lon") * lon_coarse
    own_first = lax.axis_index("lon") * lon_coarse
    summed = momentum.reshape(3, lon_coarse, 8, lat_coarse, 4, rad_coarse, 4).sum(axis=(2, 4, 6))
    viscous_sum = viscosity.reshape(lon_coarse, 8, lat_coarse, 4, rad_coarse, 4).sum(axis=(1, 3, 5))
    coarse = jnp.transpose(summed / viscous_sum[None], (1, 0, 2, 3))
    shard_piece = lax.all_gather(coarse, "lon", axis=0, tiled=True)
    sources = jnp.arange(shard_piece.shape[0], dtype=jnp.int32)
    targets = own_first + jnp.arange(lon_coarse, dtype=jnp.int32)
    kernel_table = cycle_kernel(targets[None, :] - sources[:, None], cycle_cells)
    smooth = jnp.einsum("jcyz,ji->icyz", shard_piece, kernel_table, precision=lax.Precision.HIGHEST)
    smooth = jnp.transpose(smooth, (1, 0, 2, 3))
    spread = jnp.repeat(jnp.repeat(jnp.repeat(smooth, 8, axis=1), 4, axis=2), 4, axis=3)
    velocity_out = fields[:3] + coarse_gain * spread
    pressure_out = fields[3] / viscosity
    return (velocity_out, pressure_out)


def body(velocity, pressure_in, viscosity, body_force, colour_order):
    lon_cells, lat_cells, rad_cells = viscosity.shape
    parts = lax.axis_size("lon")
    fits = (
        parts == 4
        and parts * lon_cells == 4 * SUBLANES
        and lat_cells % 4 == 0
        and lat_cells >= 2 * Y_ROWS
        and rad_cells % LANES == 0
        and rad_cells // parts + 2 * Z_MARGIN == LANES
    )
    chosen = body_windows if fits else body_general
    return chosen(velocity, pressure_in, viscosity, body_force, colour_order)


def solution(mesh):
    placed = (
        P(None, "lon", "lat", None),
        P("lon", "lat", None),
        P("lon", "lat", None),
        P(None, "lon", "lat", None),
        P(),
    )
    return jax.shard_map(
        body,
        mesh=mesh,
        in_specs=placed,
        out_specs=(P(None, "lon", "lat", None), P("lon", "lat", None)),
        check_vma=False,
    )
```
